32 devices in a mesh: grp: 2 (over y), blk: 4 (over z), head: 4 (over x, core).
Axes of the slice: x: 2, y: 2, z: 4, core: 2. Of those that a mesh axis runs over, the one named last changes fastest.
Arguments:
- queries: bfloat16 [8, 576, 4096], P('grp', None, ('head', 'blk')), parts along dimension 0, may hold values from -8 to 8
- tree_keys: bfloat16 [8, 32, 576], P('grp'), parts along dimension 0, may hold values from -8 to 8
- parents: int32 [8, 32], P('grp'), parts along dimension 0, may hold values from 0 to 30, as said below
- node_live: int32 [8, 32], P('grp'), parts along dimension 0, may hold values 0 or 1
- lengths: int32 [8], P('grp'), parts along dimension 0, may hold values from 1 to 6144, 15360 in all
- start_device: int32 [8], P('grp'), parts along dimension 0, may hold values from 0 to 3
- cache_latent: bfloat16 [8, 6144, 512], P('grp', 'blk'), parts along dimension 0, may hold values from -8 to 8
- cache_rope: bfloat16 [8, 64, 6144], P('grp', None, 'blk'), parts along dimension 0, may hold values from -8 to 8
- up_weight: bfloat16 [128, 512, 128], P('head'), may hold values from -1 to 1
Outputs:
- verified: bfloat16 [8, 32, 16384], P('grp', None, ('head', 'blk')), parts along dimension 0
The draws below stay inside these ranges and needn't reach their ends.
There are 2 independent parts, one for each index of `grp`. The reference program is written for one: setup_inputs(seed, part) draws one part's arguments, and reference() takes and returns one part's arrays. A program takes and returns all parts, laid end to end along the dimension named above; an argument that names none is the same for every part. Nothing has to cross between parts.
Inputs may be any that keep to these rules, and one draw needn't show every extreme that they name: Together the lengths fill 5/8 of the cycle's slots; one request has exactly 6144 tokens. parents[r, 0] = 0; every other node's parent has a lower index.
All inputs are finite; a program needn't handle non-finite values.
Results may differ from the reference program's by a relative error of at most 0.012.
Values may be sent and summed in bfloat16 or wider, within the bound.
A program may use at most 128 MiB of HBM per device.

```python
import math
import jax
import jax.numpy as jnp
import numpy as np
from jax import lax

DL = 512
DR = 64
DN = 128
DV = 128
HEADS = 128
NODES = 32
REQS = 4
SEG = 1536
CTX = 6144
N_BLK = 4


def draw_pair(key):
    base_key = jax.random.fold_in(key, 11)
    subkeys = jax.random.split(base_key, 3)
    query_shape = (REQS, DL + DR, HEADS * NODES)
    tree_shape = (REQS, NODES, DL + DR)
    query_vals = jnp.clip(jax.random.normal(subkeys[1], query_shape), -8.0, 8.0)
    tree_vals = jnp.clip(4.0 * jax.random.normal(subkeys[2], tree_shape), -8.0, 8.0)
    return (query_vals, tree_vals)


def draw_queries(key, part):
    return draw_pair(key)[0].astype(jnp.bfloat16)


def draw_tree_keys(key, part):
    return draw_pair(key)[1].astype(jnp.bfloat16)


def draw_parents(key, part):
    parent_key = jax.random.fold_in(key, 23)
    upper_bound = jnp.maximum(jnp.arange(NODES, dtype=jnp.int32), 1)
    drawn = jax.random.randint(parent_key, (REQS, NODES), 0, upper_bound[None, :], dtype=jnp.int32)
    return drawn.at[0, NODES - 1].set(NODES - 2)


def draw_cache_latent(key, part):
    latent_key = jax.random.fold_in(key, 41)
    base = jnp.clip(1.5 * jax.random.normal(latent_key, (REQS, CTX, DL)), -8.0, 8.0)
    return base.astype(jnp.bfloat16)


def draw_cache_rope(key, part):
    rope_key = jax.random.fold_in(key, 43)
    base = jnp.clip(1.5 * jax.random.normal(rope_key, (REQS, DR, CTX)), -8.0, 8.0)
    return base.astype(jnp.bfloat16)


def touch_ends(values, stream_key, low, largest):
    index_at = [jax.random.randint(jax.random.fold_in(stream_key, axis), (), 0, length) for axis, length in enumerate(values.shape)]
    main_axis = values.shape.index(max(values.shape))
    beside = index_at[:main_axis] + [(index_at[main_axis] + 1) % values.shape[main_axis]] + index_at[main_axis + 1:]
    return values.at[tuple(index_at)].set(low).at[tuple(beside)].set(largest)


def block_levels(key, dims, pieces, low, largest):
    factor_of, own = 1.0, jax.random.fold_in(key, 6)
    for position, blocks in pieces:
        heights = jnp.exp(jax.random.uniform(jax.random.fold_in(own, position), (blocks,), jnp.float32, low / len(pieces), largest / len(pieces)))
        factor_of = factor_of * jnp.repeat(heights, dims[position] // blocks).reshape([-1 if axis == position else 1 for axis in range(len(dims))])
    return factor_of


def profile(count, total, reach, skew):
    loads = [(1 << 20) // math.isqrt(grade ** skew) + 1 for grade in range(2, count + 1)]
    spare, given = total - reach - (count - 1), [1] * (count - 1)
    while spare > 0:
        movable = [i for i in range(count - 1) if given[i] < reach]
        whole, budget = sum([loads[i] for i in movable]), spare
        for i in movable:
            more = min(reach - given[i], max(1, budget * loads[i] // whole), spare)
            given[i] = given[i] + more
            spare = spare - more
    return np.array([reach] + given)


def ragged(key, count, total, bound, skew):
    if count == 2:
        one = jax.random.randint(key, (), max(1, total - bound), min(bound, total - 1) + 1)
        return jnp.stack([one, total - one])
    tallies = jnp.asarray(profile(count, total, bound, skew), jnp.int32)
    pairs = (count - 1) // 2
    source_of, taker = tallies[1:1 + 2 * pairs:2], tallies[2:2 + 2 * pairs:2]
    margin = jnp.minimum(source_of - 1, bound - taker)
    moved = jax.random.randint(jax.random.fold_in(key, 1), (pairs,), 0, 1 << 20) % (margin + 1)
    tallies = tallies.at[1:1 + 2 * pairs:2].set(source_of - moved).at[2:2 + 2 * pairs:2].set(taker + moved)
    return tallies[jax.random.permutation(jax.random.fold_in(key, 2), count)]


def noise(stream_key, shape, spread, bound, cuts=(), held_as=jnp.bfloat16):
    result = spread * jax.random.normal(stream_key, shape, jnp.float32)
    if cuts:
        result = result * block_levels(stream_key, shape, cuts, -0.22, 0.18)
    return jnp.clip(result, -bound, bound).astype(held_as)


def setup_inputs(seed: int = 0, part: int = 0) -> dict:
    splits = jax.random.split(jax.random.key(seed), 10)
    part_keys = jax.random.split(jax.random.fold_in(splits[9], part), 10)
    queries = draw_queries(jax.random.fold_in(jax.random.fold_in(splits[9], part), 71), part)
    tree_keys = draw_tree_keys(jax.random.fold_in(jax.random.fold_in(splits[9], part), 71), part)
    parents = draw_parents(jax.random.fold_in(jax.random.fold_in(splits[9], part), 71), part)
    node_live = touch_ends((jax.random.randint(part_keys[3], (REQS, NODES), 0, 8) < 7).astype(jnp.int32), jax.random.fold_in(part_keys[3], 1), 0, 1)
    lengths = ragged(part_keys[4], REQS, REQS * N_BLK * SEG * 5 // 8, N_BLK * SEG, 2).astype(jnp.int32)
    start_device = touch_ends(jax.random.randint(part_keys[5], (REQS,), 0, N_BLK), jax.random.fold_in(part_keys[5], 1), 0, N_BLK - 1).astype(jnp.int32)
    cache_latent = draw_cache_latent(jax.random.fold_in(jax.random.fold_in(splits[9], part), 71), part)
    cache_rope = draw_cache_rope(jax.random.fold_in(jax.random.fold_in(splits[9], part), 71), part)
    up_weight = noise(splits[8], (HEADS, DL, DV), (DL // 16) ** -0.5, 1.0, ((0, 4),))
    return {"queries": queries, "tree_keys": tree_keys, "parents": parents, "node_live": node_live, "lengths": lengths, "start_device": start_device, "cache_latent": cache_latent, "cache_rope": cache_rope, "up_weight": up_weight}


def ancestor_matrix(parent_list):
    node_count = parent_list.shape[0]
    ordering = jnp.arange(node_count, dtype=jnp.int32)
    one_hop = (parent_list[:, None] == ordering[None, :]).astype(jnp.float32)
    reached = jnp.maximum(one_hop, jnp.eye(node_count, dtype=jnp.float32))
    for repeat in range(max(node_count - 1, 1).bit_length()):
        reached = jnp.minimum(jnp.dot(reached, reached, precision=lax.Precision.HIGHEST), 1.0)
    return reached

def reference(queries, tree_keys, parents, node_live, lengths, start_device, cache_latent, cache_rope, up_weight):
    score_scale = 1.0 / math.sqrt(DN + DR)
    head_group = 8
    cycle_pages = jnp.arange(N_BLK, dtype=jnp.int32)
    key_count = N_BLK * SEG
    positions = jnp.arange(key_count, dtype=jnp.int32)
    weight_full = up_weight.astype(jnp.float32)

    def one_request(packed):
        query_all, tree_rows, parent_list, live_row, length_one, start_one, latent_all, rope_all = packed
        page_order = ((start_one + cycle_pages) % N_BLK).astype(jnp.int32)
        lat_keys = jnp.take(latent_all.reshape(N_BLK, SEG, DL), page_order, axis=0).reshape(key_count, DL)
        rope_keys = jnp.take(rope_all.reshape(DR, N_BLK, SEG), page_order, axis=1).reshape(DR, key_count)
        in_range = positions < length_one
        reached = ancestor_matrix(parent_list) > 0.5
        tree_visible = jnp.tile(reached, (head_group, 1))
        values = jnp.concatenate([tree_rows[:, :DL], lat_keys], axis=0)

        def head_block(first_col):
            query_cols = lax.dynamic_slice_in_dim(query_all, first_col, head_group * NODES, 1)
            tree_scores = jnp.dot(query_cols.T, tree_rows.T, preferred_element_type=jnp.float32) * score_scale
            ctx_scores = jnp.dot(query_cols[:DL].T, lat_keys.T, preferred_element_type=jnp.float32)
            ctx_scores = (ctx_scores + jnp.dot(query_cols[DL:].T, rope_keys, preferred_element_type=jnp.float32)) * score_scale
            scores = jnp.concatenate([jnp.where(tree_visible, tree_scores, -jnp.inf), jnp.where(in_range[None, :], ctx_scores, -jnp.inf)], axis=1)
            top_row = lax.optimization_barrier(jnp.max(scores, axis=1, keepdims=True))
            exp_scores = jnp.exp(scores - top_row)
            denominator = lax.optimization_barrier(jnp.sum(exp_scores, axis=1, keepdims=True))
            latent_out = jnp.dot(exp_scores.astype(jnp.bfloat16), values, preferred_element_type=jnp.float32)
            return latent_out / denominator
        starts = jnp.arange(HEADS // head_group, dtype=jnp.int32) * (head_group * NODES)
        latent_heads = lax.map(head_block, starts).reshape(HEADS, NODES, DL)
        projected = jnp.einsum('hnd,hdv->nhv', latent_heads, weight_full, precision=lax.Precision.HIGHEST)
        masked = projected * live_row.astype(jnp.float32)[:, None, None]
        return masked.reshape(NODES, HEADS * DV).astype(jnp.bfloat16)
    return lax.map(one_request, (queries, tree_keys, parents, node_live, lengths, start_device, cache_latent, cache_rope))
```

```python
import functools
import math

import jax
import jax.numpy as jnp
from jax import lax
from jax.experimental import pallas as pl
from jax.experimental.pallas import tpu as pltpu
from jax.sharding import PartitionSpec as P

DN = 128
NEGATIVE = -1e30
FLOOR = -1e29
LANES = 128


def kernel(
    n,
    scale,
    q_hbm,
    tree_ref,
    parent_ref,
    alive_ref,
    length_ref,
    first_ref,
    lat_hbm,
    rope_hbm,
    w_hbm,
    out_ref,
    qbuf,
    lat,
    rope,
    w,
    parts,
    mine,
    reach,
    load_sem,
    w_sem,
    q_send,
    q_recv,
    p_send,
    p_recv,
):
    me = lax.axis_index("blk")
    requests, _, cols = q_hbm.shape
    nodes = tree_ref.shape[1]
    dim_lat = lat.shape[2]
    page = lat.shape[1]
    dim_v = w.shape[2]
    heads = cols // nodes
    width = heads * dim_v

    def load_copies(r):
        return (
            pltpu.make_async_copy(q_hbm.at[r], qbuf.at[me, r], load_sem.at[0, r]),
            pltpu.make_async_copy(lat_hbm.at[r], lat.at[r], load_sem.at[1, r]),
            pltpu.make_async_copy(rope_hbm.at[r], rope.at[r], load_sem.at[2, r]),
        )

    def w_copy():
        return pltpu.make_async_copy(w_hbm, w, w_sem)

    def own_copy(r, side):
        return pltpu.make_async_remote_copy(
            src_ref=q_hbm.at[r],
            dst_ref=qbuf.at[me, r],
            send_sem=q_send.at[side, me, r],
            recv_sem=q_recv.at[me, r],
            device_id={"blk": me + 1 - 2 * side},
            device_id_type=pl.DeviceIdType.MESH,
        )

    def hop_copy(origin, r, side):
        return pltpu.make_async_remote_copy(
            src_ref=qbuf.at[origin, r],
            dst_ref=qbuf.at[origin, r],
            send_sem=q_send.at[side, origin, r],
            recv_sem=q_recv.at[origin, r],
            device_id={"blk": me + 1 - 2 * side},
            device_id_type=pl.DeviceIdType.MESH,
        )

    def part_copy(origin, r, holder):
        return pltpu.make_async_remote_copy(
            src_ref=mine.at[origin, r],
            dst_ref=parts.at[holder, r],
            send_sem=p_send.at[origin, r],
            recv_sem=p_recv.at[holder, r],
            device_id={"blk": origin},
            device_id_type=pl.DeviceIdType.MESH,
        )

    barrier = pltpu.get_barrier_semaphore()

    @pl.loop(1, n)
    def _(k):
        pl.semaphore_signal(
            barrier,
            inc=1,
            device_id={"blk": lax.rem(me + k, n)},
            device_id_type=pl.DeviceIdType.MESH,
        )

    @pl.loop(0, requests)
    def _(r):
        for copy in load_copies(r):
            copy.start()

    w_copy().start()
    pl.semaphore_wait(barrier, n - 1)

    def has_next(side):
        ahead = me + 1 - 2 * side
        return jnp.logical_and(ahead >= 0, ahead < n)

    @pl.loop(0, requests)
    def _(r):
        for side in (0, 1):

            @pl.when(has_next(side))
            def _():
                own_copy(r, side).start()

    total = requests * nodes
    order = lax.broadcasted_iota(jnp.int32, (total, total), 1)
    row = lax.broadcasted_iota(jnp.int32, (total, total), 0)
    reached = jnp.where(jnp.logical_or(parent_ref[...] == order, row == order), 1.0, 0.0)
    for _ in range(max(nodes - 1, 1).bit_length()):
        factor = reached.astype(jnp.bfloat16)
        reached = jnp.minimum(jnp.dot(factor, factor, preferred_element_type=jnp.float32), 1.0)
    reach[...] = reached.reshape(requests, nodes, total)

    def stats(scores, values):
        top = jnp.maximum(jnp.max(scores, axis=1, keepdims=True), FLOOR)
        weights = jnp.exp2(scores - top)
        summed = jnp.sum(weights, axis=1, keepdims=True)
        acc = jnp.dot(weights.astype(jnp.bfloat16), values, preferred_element_type=jnp.float32)
        return top, summed, acc

    def page_scores(q, r):
        s = lax.dot_general(
            q[:, :dim_lat], lat[r], (((1,), (1,)), ((), ())), preferred_element_type=jnp.float32
        )
        s = s + jnp.dot(q[:, dim_lat:], rope[r], preferred_element_type=jnp.float32)
        turn = lax.rem(me - first_ref[r] + n, n)
        live = length_ref[r] - turn * page
        slot = lax.broadcasted_iota(jnp.int32, (1, page), 1)
        return jnp.where(slot < live, s * scale, NEGATIVE)

    def finish(top, summed, acc, origin, dst):
        kept = summed > 0.0
        inverse = jnp.where(kept, 1.0 / jnp.where(kept, summed, 1.0), 0.0)
        rows = (acc * inverse).astype(jnp.bfloat16)
        lse = jnp.where(kept, top + jnp.log2(jnp.where(kept, summed, 1.0)), NEGATIVE)
        lane = lax.broadcasted_iota(jnp.int32, (nodes, LANES), 1)
        stat = jnp.zeros((nodes, LANES), jnp.float32)
        for h in range(heads):
            span = slice(h * nodes, (h + 1) * nodes)
            projected = jnp.dot(
                rows[span], w[origin * heads + h], preferred_element_type=jnp.float32
            )
            dst[:, h * dim_v : (h + 1) * dim_v] = projected.astype(jnp.bfloat16)
            stat = jnp.where(lane % heads == h, lse[span], stat)
        high = stat.astype(jnp.bfloat16)
        rest = stat - high.astype(jnp.float32)
        middle = rest.astype(jnp.bfloat16)
        low = (rest - middle.astype(jnp.float32)).astype(jnp.bfloat16)
        packed = jnp.where(
            lane < heads,
            high.astype(jnp.float32),
            jnp.where(lane < 2 * heads, middle.astype(jnp.float32), low.astype(jnp.float32)),
        )
        dst[:, width : width + LANES] = packed.astype(jnp.bfloat16)

    w_copy().wait()

    @pl.loop(0, requests)
    def _(r):
        for copy in load_copies(r):
            copy.wait()
        q = qbuf[me, r].T
        top, summed, acc = stats(page_scores(q, r), lat[r])
        keys = tree_ref[...].reshape(total, tree_ref.shape[2])
        s = lax.dot_general(
            q, keys, (((1,), (1,)), ((), ())), preferred_element_type=jnp.float32
        )
        seen = jnp.concatenate([reach[r]] * heads, axis=0) > 0.5
        s = jnp.where(seen, s * scale, NEGATIVE)
        top_t, summed_t, acc_t = stats(s, keys[:, :dim_lat])
        both = jnp.maximum(top, top_t)
        f, f_t = jnp.exp2(top - both), jnp.exp2(top_t - both)
        finish(both, summed * f + summed_t * f_t, acc * f + acc_t * f_t, me, parts.at[me, r])

    def place(t):
        d = t // (2 * requests) + 1
        r = lax.rem(t // 2, requests)
        side = lax.rem(t, 2)
        origin = me - d + 2 * d * side
        return origin, r, side, jnp.logical_and(origin >= 0, origin < n)

    steps = 2 * requests * (n - 1)

    @pl.loop(0, steps)
    def _(t):
        origin, r, side, valid = place(t)

        @pl.when(valid)
        def _():
            hop_copy(origin, r, side).wait_recv()

            @pl.when(has_next(side))
            def _():
                hop_copy(origin, r, side).start()

            q = qbuf[origin, r].T
            top, summed, acc = stats(page_scores(q, r), lat[r])
            finish(top, summed, acc, origin, mine.at[origin, r])
            part_copy(origin, r, me).start()

    lane = lax.broadcasted_iota(jnp.int32, (nodes, LANES), 1)

    @pl.loop(0, requests)
    def _(r):
        @pl.loop(1, n)
        def _(k):
            part_copy(me, r, lax.rem(me + k, n)).wait_recv()

        def lse_of(slot):
            stat = parts[slot, r, :, width : width + LANES].astype(jnp.float32)
            lse = stat + pltpu.roll(stat, LANES - heads, 1) + pltpu.roll(stat, LANES - 2 * heads, 1)
            return jnp.where(lane < heads, lse, NEGATIVE)

        top = lax.fori_loop(
            1, n, lambda k, best: jnp.maximum(best, lse_of(k)), lse_of(0), unroll=n <= 8
        )
        top = jnp.where(lane < heads, top, 0.0)

        def add(k, carried):
            weight_sum, summed = carried
            weight = jnp.exp2(lse_of(k) - top)
            spread = jnp.concatenate(
                [jnp.broadcast_to(weight[:, h : h + 1], (nodes, dim_v)) for h in range(heads)], axis=1
            )
            return (
                weight_sum + spread,
                summed + spread * parts[k, r, :, :width].astype(jnp.float32),
            )

        zero = jnp.zeros((nodes, width), jnp.float32)
        weight_sum, summed = lax.fori_loop(0, n, add, (zero, zero), unroll=n <= 8)
        out_ref[r] = (summed / weight_sum * alive_ref[r]).astype(out_ref.dtype)

    @pl.loop(0, requests)
    def _(r):
        for side in (0, 1):

            @pl.when(has_next(side))
            def _():
                own_copy(r, side).wait_send()

    @pl.loop(0, steps)
    def _(t):
        origin, r, side, valid = place(t)

        @pl.when(valid)
        def _():
            @pl.when(has_next(side))
            def _():
                hop_copy(origin, r, side).wait_send()

            part_copy(origin, r, me).wait_send()


def shards(
    queries,
    tree_keys,
    parents,
    node_live,
    lengths,
    start_device,
    cache_latent,
    cache_rope,
    up_weight,
):
    n = lax.axis_size("blk")
    requests, dim_q, cols = queries.shape
    nodes = tree_keys.shape[1]
    _, page, dim_lat = cache_latent.shape
    dim_rope = cache_rope.shape[1]
    dim_v = up_weight.shape[2]
    width = cols // nodes * dim_v
    bf16 = jnp.bfloat16
    scale = math.log2(math.e) / math.sqrt(DN + dim_rope)
    shift = jnp.arange(requests, dtype=jnp.int32)[:, None] * nodes
    parent = (parents + shift).reshape(requests * nodes, 1)
    alive = node_live.astype(jnp.float32)[:, :, None]
    vmem = pl.BlockSpec(memory_space=pltpu.VMEM)
    smem = pl.BlockSpec(memory_space=pltpu.SMEM)
    anywhere = pl.BlockSpec(memory_space=pl.ANY)
    return pl.pallas_call(
        functools.partial(kernel, n, scale),
        out_shape=jax.ShapeDtypeStruct((requests, nodes, width), bf16),
        in_specs=[anywhere, vmem, vmem, vmem, smem, smem, anywhere, anywhere, anywhere],
        out_specs=vmem,
        scratch_shapes=[
            pltpu.VMEM((n, requests, dim_q, cols), bf16),
            pltpu.VMEM((requests, page, dim_lat), bf16),
            pltpu.VMEM((requests, dim_rope, page), bf16),
            pltpu.VMEM(up_weight.shape, bf16),
            pltpu.VMEM((n, requests, nodes, width + LANES), bf16),
            pltpu.VMEM((n, requests, nodes, width + LANES), bf16),
            pltpu.VMEM((requests, nodes, requests * nodes), jnp.float32),
            pltpu.SemaphoreType.DMA((3, requests)),
            pltpu.SemaphoreType.DMA,
            pltpu.SemaphoreType.DMA((2, n, requests)),
            pltpu.SemaphoreType.DMA((n, requests)),
            pltpu.SemaphoreType.DMA((n, requests)),
            pltpu.SemaphoreType.DMA((n, requests)),
        ],
        compiler_params=pltpu.CompilerParams(
            collective_id=0, has_side_effects=True, vmem_limit_bytes=60 * 1024 * 1024
        ),
        name="tree_attention",
    )(
        queries,
        tree_keys,
        parent,
        alive,
        lengths,
        start_device,
        cache_latent,
        cache_rope,
        up_weight,
    )


def solution(mesh):
    return jax.shard_map(
        shards,
        mesh=mesh,
        in_specs=(
            P("grp", None, ("head", "blk")),
            P("grp", None, None),
            P("grp", None),
            P("grp", None),
            P("grp"),
            P("grp"),
            P("grp", "blk", None),
            P("grp", None, "blk"),
            P("head", None, None),
        ),
        out_specs=P("grp", None, ("head", "blk")),
        check_vma=False,
    )
```

```python
import functools
import math

import jax
import jax.numpy as jnp
from jax import lax
from jax.experimental import pallas as pl
from jax.experimental.pallas import tpu as pltpu
from jax.sharding import PartitionSpec as P

DN = 128
NEGATIVE = -1e30
FLOOR = -1e29
LANES = 128


def kernel(
    n,
    peers,
    moved,
    scale,
    q_hbm,
    tree_ref,
    parent_ref,
    alive_ref,
    length_ref,
    first_ref,
    lat_hbm,
    rope_hbm,
    w_hbm,
    out_ref,
    qbuf,
    lat,
    rope,
    w,
    parts,
    mine,
    reach,
    top_ref,
    sum_ref,
    acc_ref,
    load_sem,
    w_sem,
    q_send,
    q_recv,
    p_send,
    p_recv,
    page_send,
    peer_send,
    page_recv,
):
    me = lax.axis_index("blk")
    lane_me = lax.axis_index("head")
    requests, _, cols = q_hbm.shape
    nodes = tree_ref.shape[1]
    dim_lat = lat.shape[2]
    page = lat.shape[1]
    dim_v = w.shape[2]
    heads = cols // nodes
    width = heads * dim_v
    kept = requests - moved
    share = page // peers
    mesh_id = pl.DeviceIdType.MESH
    at_end = jnp.logical_or(me == 0, me == n - 1)
    near_end = jnp.logical_or(me == 1, me == n - 2)
    end_side = jnp.where(me <= 1, 0, n - 1)

    def load_copies(r):
        return (
            pltpu.make_async_copy(q_hbm.at[r], qbuf.at[me, r], load_sem.at[0, r]),
            pltpu.make_async_copy(lat_hbm.at[r], lat.at[r], load_sem.at[1, r]),
            pltpu.make_async_copy(rope_hbm.at[r], rope.at[r], load_sem.at[2, r]),
        )

    def w_copy():
        return pltpu.make_async_copy(w_hbm, w, w_sem)

    def own_copy(r, side):
        return pltpu.make_async_remote_copy(
            src_ref=q_hbm.at[r],
            dst_ref=qbuf.at[me, r],
            send_sem=q_send.at[side, me, r],
            recv_sem=q_recv.at[me, r],
            device_id={"blk": me + 1 - 2 * side},
            device_id_type=mesh_id,
        )

    def hop_copy(origin, r, side):
        return pltpu.make_async_remote_copy(
            src_ref=qbuf.at[origin, r],
            dst_ref=qbuf.at[origin, r],
            send_sem=q_send.at[side, origin, r],
            recv_sem=q_recv.at[origin, r],
            device_id={"blk": me + 1 - 2 * side},
            device_id_type=mesh_id,
        )

    def part_copy(origin, r, holder):
        return pltpu.make_async_remote_copy(
            src_ref=mine.at[origin, r],
            dst_ref=parts.at[holder, r],
            send_sem=p_send.at[origin, r],
            recv_sem=p_recv.at[holder, r],
            device_id={"blk": origin},
            device_id_type=mesh_id,
        )

    def rows_of(j):
        return pl.ds(pl.multiple_of(j * share, share), share)

    def page_copies(g):
        inner = jnp.where(me == 0, 1, n - 2)
        mine_rows = rows_of(lane_me)
        return (
            pltpu.make_async_remote_copy(
                src_ref=lat_hbm.at[kept + g, mine_rows],
                dst_ref=lat.at[requests + g, mine_rows],
                send_sem=page_send.at[0, g],
                recv_sem=page_recv.at[0, g, lane_me],
                device_id={"blk": inner},
                device_id_type=mesh_id,
            ),
            pltpu.make_async_remote_copy(
                src_ref=rope_hbm.at[kept + g, :, mine_rows],
                dst_ref=rope.at[requests + g, :, mine_rows],
                send_sem=page_send.at[1, g],
                recv_sem=page_recv.at[1, g, lane_me],
                device_id={"blk": inner},
                device_id_type=mesh_id,
            ),
        )

    def peer_copies(g, j, peer):
        share_rows = rows_of(j)
        return tuple(
            pltpu.make_async_remote_copy(
                src_ref=view,
                dst_ref=view,
                send_sem=peer_send.at[i, g, peer],
                recv_sem=page_recv.at[i, g, j],
                device_id={"head": peer},
                device_id_type=mesh_id,
            )
            for i, view in enumerate(
                (lat.at[requests + g, share_rows], rope.at[requests + g, :, share_rows])
            )
        )

    barrier = pltpu.get_barrier_semaphore()

    @pl.loop(1, n)
    def _(k):
        pl.semaphore_signal(
            barrier, inc=1, device_id={"blk": lax.rem(me + k, n)}, device_id_type=mesh_id
        )

    if moved:

        @pl.loop(1, peers)
        def _(k):
            pl.semaphore_signal(
                barrier,
                inc=1,
                device_id={"head": lax.rem(lane_me + k, peers)},
                device_id_type=mesh_id,
            )

    @pl.loop(0, requests)
    def _(r):
        for copy in load_copies(r):
            copy.start()

    w_copy().start()
    pl.semaphore_wait(barrier, n - 1 + (peers - 1 if moved else 0))

    def sends_on(r, side):
        ahead = me + 1 - 2 * side
        valid = jnp.logical_and(ahead >= 0, ahead < n)
        if moved:
            last = jnp.logical_or(ahead == 0, ahead == n - 1)
            valid = jnp.logical_and(valid, jnp.logical_not(jnp.logical_and(last, r >= kept)))
        return valid

    if moved:

        @pl.when(at_end)
        def _():
            @pl.loop(0, moved)
            def _(g):
                for copy in page_copies(g):
                    copy.start()

    @pl.loop(0, requests)
    def _(r):
        for side in (0, 1):

            @pl.when(sends_on(r, side))
            def _():
                own_copy(r, side).start()

    lane = lax.broadcasted_iota(jnp.int32, (nodes, LANES), 1)
    total = requests * nodes
    column = lax.broadcasted_iota(jnp.int32, (total, total), 1)
    row = lax.broadcasted_iota(jnp.int32, (total, total), 0)
    parent = jnp.concatenate(
        [parent_ref[r : r + 1, :] + r * nodes for r in range(requests)], axis=1
    )
    reached = jnp.where(jnp.logical_or(parent == row, row == column), 1.0, 0.0)
    for _ in range(max(nodes - 1, 1).bit_length()):
        factor = reached.astype(jnp.bfloat16)
        reached = jnp.minimum(jnp.dot(factor, factor, preferred_element_type=jnp.float32), 1.0)
    reach[...] = reached.T.reshape(requests, nodes, total)

    if moved:
        for end in (0, n - 1):

            @pl.when(me != end)
            def _():
                @pl.loop(0, moved)
                def _(g):
                    blank = parts.at[end, kept + g]
                    blank[:, :width] = jnp.zeros((nodes, width), jnp.bfloat16)
                    blank[:, width:] = jnp.where(lane < heads, NEGATIVE, 0.0).astype(jnp.bfloat16)

    def stats(scores, values):
        top = jnp.maximum(jnp.max(scores, axis=1, keepdims=True), FLOOR)
        weights = jnp.exp2(scores - top)
        summed = jnp.sum(weights, axis=1, keepdims=True)
        acc = jnp.dot(weights.astype(jnp.bfloat16), values, preferred_element_type=jnp.float32)
        return top, summed, acc

    def page_scores(q, place, r, holder):
        s = lax.dot_general(
            q[:, :dim_lat], lat[place], (((1,), (1,)), ((), ())), preferred_element_type=jnp.float32
        )
        s = s + jnp.dot(q[:, dim_lat:], rope[place], preferred_element_type=jnp.float32)
        turn = lax.rem(holder - first_ref[r] + n, n)
        live = length_ref[r] - turn * page
        slot = lax.broadcasted_iota(jnp.int32, (1, page), 1)
        return jnp.where(slot < live, s * scale, NEGATIVE)

    def finish(top, summed, acc, origin, dst):
        any_kept = summed > 0.0
        safe = jnp.where(any_kept, summed, 1.0)
        rows = (acc * jnp.where(any_kept, 1.0 / safe, 0.0)).astype(jnp.bfloat16)
        lse = jnp.where(any_kept, top + jnp.log2(safe), NEGATIVE)
        stat = jnp.zeros((nodes, LANES), jnp.float32)
        for h in range(heads):
            span = slice(h * nodes, (h + 1) * nodes)
            projected = jnp.dot(
                rows[span], w[origin * heads + h], preferred_element_type=jnp.float32
            )
            dst[:, h * dim_v : (h + 1) * dim_v] = projected.astype(jnp.bfloat16)
            stat = jnp.where(lane % heads == h, lse[span], stat)
        high = stat.astype(jnp.bfloat16)
        rest = stat - high.astype(jnp.float32)
        middle = rest.astype(jnp.bfloat16)
        low = (rest - middle.astype(jnp.float32)).astype(jnp.bfloat16)
        packed = jnp.where(
            lane < heads,
            high.astype(jnp.float32),
            jnp.where(lane < 2 * heads, middle.astype(jnp.float32), low.astype(jnp.float32)),
        )
        dst[:, width : width + LANES] = packed.astype(jnp.bfloat16)

    w_copy().wait()

    @pl.loop(0, requests)
    def _(r):
        for copy in load_copies(r):
            copy.wait()
        q = qbuf[me, r].T
        keys = tree_ref[...].reshape(total, tree_ref.shape[2])
        s = lax.dot_general(q, keys, (((1,), (1,)), ((), ())), preferred_element_type=jnp.float32)
        seen = jnp.concatenate([reach[r]] * heads, axis=0) > 0.5
        s = jnp.where(seen, s * scale, NEGATIVE)
        top, summed, acc = stats(s, keys[:, :dim_lat])
        finish(top, summed, acc, me, parts.at[me, r])

    near = 2 * requests
    steps = near * (n - 1) + requests

    def place(u):
        v = u - kept
        late = v >= near
        own = jnp.logical_or(v < 0, jnp.logical_and(late, v < near + moved))
        t = jnp.where(late, v - moved, jnp.maximum(v, 0))
        d = t // near + 1
        side = lax.rem(t, 2)
        r = jnp.where(
            own, jnp.where(late, kept + v - near, u), lax.rem(t // 2, requests)
        )
        origin = jnp.where(own, me, me - d + 2 * d * side)
        valid = jnp.logical_and(origin >= 0, origin < n)
        if moved:
            skipped = jnp.logical_and(jnp.logical_not(own), jnp.logical_and(at_end, r >= kept))
            valid = jnp.logical_and(valid, jnp.logical_not(skipped))
        return origin, r, side, jnp.logical_not(own), valid

    @pl.loop(0, steps)
    def _(u):
        origin, r, side, foreign, valid = place(u)

        if moved:

            @pl.when(jnp.logical_and(near_end, u == kept))
            def _():
                @pl.loop(0, moved)
                def _(g):
                    for copy in peer_copies(g, lane_me, lane_me):
                        copy.wait_recv()

                    @pl.loop(1, peers)
                    def _(k):
                        for copy in peer_copies(g, lane_me, lax.rem(lane_me + k, peers)):
                            copy.start()

            @pl.when(jnp.logical_and(near_end, u == 3 * kept))
            def _():
                @pl.loop(0, moved)
                def _(g):
                    @pl.loop(1, peers)
                    def _(k):
                        j = lax.rem(lane_me + k, peers)
                        for copy in peer_copies(g, j, lane_me):
                            copy.wait_recv()

        @pl.when(jnp.logical_and(foreign, valid))
        def _():
            hop_copy(origin, r, side).wait_recv()

            @pl.when(sends_on(r, side))
            def _():
                hop_copy(origin, r, side).start()

        @pl.when(valid)
        def _():
            q = qbuf[origin, r].T
            top, summed, acc = stats(page_scores(q, r, r, me), lat[r])
            top_ref[...] = top
            sum_ref[...] = summed
            acc_ref[...] = acc
            if moved:
                away = jnp.logical_and(near_end, jnp.logical_and(r >= kept, origin != end_side))

                @pl.when(away)
                def _():
                    extra = r + moved
                    top_x, sum_x, acc_x = stats(page_scores(q, extra, r, end_side), lat[extra])
                    top_a = top_ref[...]
                    both = jnp.maximum(top_a, top_x)
                    f_a, f_x = jnp.exp2(top_a - both), jnp.exp2(top_x - both)
                    top_ref[...] = both
                    sum_ref[...] = sum_ref[...] * f_a + sum_x * f_x
                    acc_ref[...] = acc_ref[...] * f_a + acc_x * f_x

            finish(top_ref[...], sum_ref[...], acc_ref[...], origin, mine.at[origin, r])

            @pl.when(foreign)
            def _():
                part_copy(origin, r, me).start()

    def arrives(r, holder):
        if not moved:
            return None
        last = jnp.logical_or(holder == 0, holder == n - 1)
        return jnp.logical_not(jnp.logical_and(last, r >= kept))

    eye = lax.broadcasted_iota(jnp.int32, (nodes, nodes), 0) == lax.broadcasted_iota(
        jnp.int32, (nodes, nodes), 1
    )

    @pl.loop(0, requests)
    def _(r):
        @pl.loop(1, n)
        def _(k):
            holder = lax.rem(me + k, n)
            if moved:

                @pl.when(arrives(r, holder))
                def _():
                    part_copy(me, r, holder).wait_recv()

            else:
                part_copy(me, r, holder).wait_recv()

        def lse_of(stat):
            stat = stat.astype(jnp.float32)
            lse = stat + pltpu.roll(stat, LANES - heads, 1) + pltpu.roll(stat, LANES - 2 * heads, 1)
            return jnp.where(lane < heads, lse, NEGATIVE)

        own = mine[me, r]
        own_lse = lse_of(own[:, width:])
        top = lax.fori_loop(
            0,
            n,
            lambda k, best: jnp.maximum(best, lse_of(parts[k, r, :, width : width + LANES])),
            own_lse,
            unroll=n <= 8,
        )
        top = jnp.where(lane < heads, top, 0.0)

        def add(carried, lse, part):
            weight_sum, summed = carried
            weight = jnp.exp2(lse - top)
            spread = jnp.concatenate(
                [jnp.broadcast_to(weight[:, h : h + 1], (nodes, dim_v)) for h in range(heads)], axis=1
            )
            return weight_sum + spread, summed + spread * part.astype(jnp.float32)

        zero = jnp.zeros((nodes, width), jnp.float32)
        weight_sum, summed = lax.fori_loop(
            0,
            n,
            lambda k, carried: add(
                carried, lse_of(parts[k, r, :, width : width + LANES]), parts[k, r, :, :width]
            ),
            add((zero, zero), own_lse, own[:, :width]),
            unroll=n <= 8,
        )
        alive = alive_ref[pl.ds(r, 1), :].astype(jnp.float32)
        alive = jnp.sum(jnp.where(eye, alive, 0.0), axis=1, keepdims=True)
        out_ref[r] = (summed / weight_sum * alive).astype(out_ref.dtype)

    if moved:

        @pl.when(at_end)
        def _():
            @pl.loop(0, moved)
            def _(g):
                for copy in page_copies(g):
                    copy.wait_send()

        @pl.when(near_end)
        def _():
            @pl.loop(0, moved)
            def _(g):
                @pl.loop(1, peers)
                def _(k):
                    for copy in peer_copies(g, lane_me, lax.rem(lane_me + k, peers)):
                        copy.wait_send()

    @pl.loop(0, requests)
    def _(r):
        for side in (0, 1):

            @pl.when(sends_on(r, side))
            def _():
                own_copy(r, side).wait_send()

    @pl.loop(0, steps)
    def _(u):
        origin, r, side, foreign, valid = place(u)

        @pl.when(jnp.logical_and(foreign, valid))
        def _():
            @pl.when(sends_on(r, side))
            def _():
                hop_copy(origin, r, side).wait_send()

            part_copy(origin, r, me).wait_send()


def shards(
    queries,
    tree_keys,
    parents,
    node_live,
    lengths,
    start_device,
    cache_latent,
    cache_rope,
    up_weight,
):
    n = lax.axis_size("blk")
    requests, dim_q, cols = queries.shape
    nodes = tree_keys.shape[1]
    _, page, dim_lat = cache_latent.shape
    dim_rope = cache_rope.shape[1]
    dim_v = up_weight.shape[2]
    width = cols // nodes * dim_v
    bf16 = jnp.bfloat16
    scale = math.log2(math.e) / math.sqrt(DN + dim_rope)
    peers = lax.axis_size("head")
    movable = n >= 4 and page % (peers * LANES) == 0
    moved = max(requests // 4, 1) if movable else 0
    slots = max(moved, 1)
    vmem = pl.BlockSpec(memory_space=pltpu.VMEM)
    smem = pl.BlockSpec(memory_space=pltpu.SMEM)
    anywhere = pl.BlockSpec(memory_space=pl.ANY)
    return pl.pallas_call(
        functools.partial(kernel, n, peers, moved, scale),
        out_shape=jax.ShapeDtypeStruct((requests, nodes, width), bf16),
        in_specs=[anywhere, vmem, vmem, vmem, smem, smem, anywhere, anywhere, anywhere],
        out_specs=vmem,
        scratch_shapes=[
            pltpu.VMEM((n, requests, dim_q, cols), bf16),
            pltpu.VMEM((requests + moved, page, dim_lat), bf16),
            pltpu.VMEM((requests + moved, dim_rope, page), bf16),
            pltpu.VMEM(up_weight.shape, bf16),
            pltpu.VMEM((n, requests, nodes, width + LANES), bf16),
            pltpu.VMEM((n, requests, nodes, width + LANES), bf16),
            pltpu.VMEM((requests, nodes, requests * nodes), jnp.float32),
            pltpu.VMEM((cols, 1), jnp.float32),
            pltpu.VMEM((cols, 1), jnp.float32),
            pltpu.VMEM((cols, dim_lat), jnp.float32),
            pltpu.SemaphoreType.DMA((3, requests)),
            pltpu.SemaphoreType.DMA,
            pltpu.SemaphoreType.DMA((2, n, requests)),
            pltpu.SemaphoreType.DMA((n, requests)),
            pltpu.SemaphoreType.DMA((n, requests)),
            pltpu.SemaphoreType.DMA((n, requests)),
            pltpu.SemaphoreType.DMA((2, slots)),
            pltpu.SemaphoreType.DMA((2, slots, peers)),
            pltpu.SemaphoreType.DMA((2, slots, peers)),
        ],
        compiler_params=pltpu.CompilerParams(
            collective_id=0, has_side_effects=True, vmem_limit_bytes=60 * 1024 * 1024
        ),
        name="tree_attention",
    )(
        queries,
        tree_keys,
        parents,
        node_live,
        lengths,
        start_device,
        cache_latent,
        cache_rope,
        up_weight,
    )


def solution(mesh):
    return jax.shard_map(
        shards,
        mesh=mesh,
        in_specs=(
            P("grp", None, ("head", "blk")),
            P("grp", None, None),
            P("grp", None),
            P("grp", None),
            P("grp"),
            P("grp"),
            P("grp", "blk", None),
            P("grp", None, "blk"),
            P("head", None, None),
        ),
        out_specs=P("grp", None, ("head", "blk")),
        check_vma=False,
    )
```

```python
import functools
import math

import jax
import jax.numpy as jnp
from jax import lax
from jax.experimental import pallas as pl
from jax.experimental.pallas import tpu as pltpu
from jax.sharding import PartitionSpec as P

DN = 128
NEGATIVE = -1e30
FLOOR = -1e29
LANES = 128


def kernel(
    n,
    peers,
    moved,
    scale,
    q_hbm,
    tree_ref,
    parent_ref,
    alive_ref,
    length_ref,
    first_ref,
    lat_hbm,
    rope_hbm,
    w_hbm,
    out_ref,
    qbuf,
    lat,
    rope,
    w,
    parts,
    mine,
    reach,
    top_ref,
    sum_ref,
    acc_ref,
    load_sem,
    w_sem,
    q_send,
    q_recv,
    p_send,
    p_recv,
    page_send,
    peer_send,
    page_recv,
):
    me = lax.axis_index("blk")
    lane_me = lax.axis_index("head")
    requests, _, cols = q_hbm.shape
    nodes = tree_ref.shape[1]
    dim_lat = lat.shape[2]
    page = lat.shape[1]
    dim_v = w.shape[2]
    heads = cols // nodes
    width = heads * dim_v
    kept = requests - moved
    share = page // peers
    mesh_id = pl.DeviceIdType.MESH
    at_end = jnp.logical_or(me == 0, me == n - 1)
    near_end = jnp.logical_or(me == 1, me == n - 2)
    end_side = jnp.where(me <= 1, 0, n - 1)

    def load_copies(r):
        return (
            pltpu.make_async_copy(q_hbm.at[r], qbuf.at[me, r], load_sem.at[0, r]),
            pltpu.make_async_copy(lat_hbm.at[r], lat.at[r], load_sem.at[1, r]),
            pltpu.make_async_copy(rope_hbm.at[r], rope.at[r], load_sem.at[2, r]),
        )

    def w_copy():
        return pltpu.make_async_copy(w_hbm, w, w_sem)

    def own_copy(r, side):
        return pltpu.make_async_remote_copy(
            src_ref=q_hbm.at[r],
            dst_ref=qbuf.at[me, r],
            send_sem=q_send.at[side, me, r],
            recv_sem=q_recv.at[me, r],
            device_id={"blk": me + 1 - 2 * side},
            device_id_type=mesh_id,
        )

    def hop_copy(origin, r, side):
        return pltpu.make_async_remote_copy(
            src_ref=qbuf.at[origin, r],
            dst_ref=qbuf.at[origin, r],
            send_sem=q_send.at[side, origin, r],
            recv_sem=q_recv.at[origin, r],
            device_id={"blk": me + 1 - 2 * side},
            device_id_type=mesh_id,
        )

    def part_copy(origin, r, holder):
        return pltpu.make_async_remote_copy(
            src_ref=mine.at[origin, r],
            dst_ref=parts.at[holder, r],
            send_sem=p_send.at[origin, r],
            recv_sem=p_recv.at[holder, r],
            device_id={"blk": origin},
            device_id_type=mesh_id,
        )

    def rows_of(j):
        return pl.ds(pl.multiple_of(j * share, share), share)

    def page_copies(g):
        inner = jnp.where(me == 0, 1, n - 2)
        mine_rows = rows_of(lane_me)
        return (
            pltpu.make_async_remote_copy(
                src_ref=lat_hbm.at[kept + g, mine_rows],
                dst_ref=lat.at[requests + g, mine_rows],
                send_sem=page_send.at[0, g],
                recv_sem=page_recv.at[0, g, lane_me],
                device_id={"blk": inner},
                device_id_type=mesh_id,
            ),
            pltpu.make_async_remote_copy(
                src_ref=rope_hbm.at[kept + g, :, mine_rows],
                dst_ref=rope.at[requests + g, :, mine_rows],
                send_sem=page_send.at[1, g],
                recv_sem=page_recv.at[1, g, lane_me],
                device_id={"blk": inner},
                device_id_type=mesh_id,
            ),
        )

    stages = []
    while moved and (peers >> len(stages)) > 1:
        stages.append(peers >> (len(stages) + 1))

    def partner(j, gap):
        return j + gap * (1 - 2 * lax.rem(j // gap, 2))

    def held(stage):
        slices = [lane_me]
        for gap in stages[:stage]:
            slices = slices + [partner(j, gap) for j in slices]
        return slices

    def share_copies(g, stage):
        target = partner(lane_me, stages[stage])
        pieces = held(stage)
        return [
            pltpu.make_async_remote_copy(
                src_ref=view,
                dst_ref=view,
                send_sem=peer_send.at[i, g, len(pieces) - 1 + at],
                recv_sem=page_recv.at[i, g, j],
                device_id={"head": target},
                device_id_type=mesh_id,
            )
            for at, j in enumerate(pieces)
            for i, view in enumerate(
                (lat.at[requests + g, rows_of(j)], rope.at[requests + g, :, rows_of(j)])
            )
        ]

    def await_pieces(g, pieces):
        for j in pieces:
            for i, view in enumerate(
                (lat.at[requests + g, rows_of(j)], rope.at[requests + g, :, rows_of(j)])
            ):
                pltpu.make_async_remote_copy(
                    src_ref=view,
                    dst_ref=view,
                    send_sem=page_send.at[i, g],
                    recv_sem=page_recv.at[i, g, j],
                    device_id={"blk": me},
                    device_id_type=mesh_id,
                ).wait_recv()

    def share_stage(g, stage):
        pieces = held(stage)
        await_pieces(g, pieces[len(pieces) // 2 :])
        if stage < len(stages):
            for copy in share_copies(g, stage):
                copy.start()

    barrier = pltpu.get_barrier_semaphore()

    @pl.loop(1, n)
    def _(k):
        pl.semaphore_signal(
            barrier, inc=1, device_id={"blk": lax.rem(me + k, n)}, device_id_type=mesh_id
        )

    if moved:

        @pl.loop(1, peers)
        def _(k):
            pl.semaphore_signal(
                barrier,
                inc=1,
                device_id={"head": lax.rem(lane_me + k, peers)},
                device_id_type=mesh_id,
            )

    @pl.loop(0, requests)
    def _(r):
        for copy in load_copies(r):
            copy.start()

    w_copy().start()
    pl.semaphore_wait(barrier, n - 1 + (peers - 1 if moved else 0))

    def sends_on(r, side):
        ahead = me + 1 - 2 * side
        valid = jnp.logical_and(ahead >= 0, ahead < n)
        if moved:
            last = jnp.logical_or(ahead == 0, ahead == n - 1)
            valid = jnp.logical_and(valid, jnp.logical_not(jnp.logical_and(last, r >= kept)))
        return valid

    if moved:

        @pl.when(at_end)
        def _():
            @pl.loop(0, moved)
            def _(g):
                for copy in page_copies(g):
                    copy.start()

    @pl.loop(0, requests)
    def _(r):
        for side in (0, 1):

            @pl.when(sends_on(r, side))
            def _():
                own_copy(r, side).start()

    lane = lax.broadcasted_iota(jnp.int32, (nodes, LANES), 1)
    total = requests * nodes
    column = lax.broadcasted_iota(jnp.int32, (total, total), 1)
    row = lax.broadcasted_iota(jnp.int32, (total, total), 0)
    parent = jnp.concatenate(
        [parent_ref[r : r + 1, :] + r * nodes for r in range(requests)], axis=1
    )
    reached = jnp.where(jnp.logical_or(parent == row, row == column), 1.0, 0.0)
    for _ in range(max(nodes - 1, 1).bit_length()):
        factor = reached.astype(jnp.bfloat16)
        reached = jnp.minimum(jnp.dot(factor, factor, preferred_element_type=jnp.float32), 1.0)
    reach[...] = reached.T.reshape(requests, nodes, total)

    if moved:
        for end in (0, n - 1):

            @pl.when(me != end)
            def _():
                @pl.loop(0, moved)
                def _(g):
                    blank = parts.at[end, kept + g]
                    blank[:, :width] = jnp.zeros((nodes, width), jnp.bfloat16)
                    blank[:, width:] = jnp.where(lane < heads, NEGATIVE, 0.0).astype(jnp.bfloat16)

    def stats(scores, values):
        top = jnp.maximum(jnp.max(scores, axis=1, keepdims=True), FLOOR)
        weights = jnp.exp2(scores - top)
        summed = jnp.sum(weights, axis=1, keepdims=True)
        acc = jnp.dot(weights.astype(jnp.bfloat16), values, preferred_element_type=jnp.float32)
        return top, summed, acc

    def page_scores(q, place, r, holder):
        s = lax.dot_general(
            q[:, :dim_lat], lat[place], (((1,), (1,)), ((), ())), preferred_element_type=jnp.float32
        )
        s = s + jnp.dot(q[:, dim_lat:], rope[place], preferred_element_type=jnp.float32)
        turn = lax.rem(holder - first_ref[r] + n, n)
        live = length_ref[r] - turn * page
        slot = lax.broadcasted_iota(jnp.int32, (1, page), 1)
        return jnp.where(slot < live, s * scale, NEGATIVE)

    def finish(top, summed, acc, origin, dst):
        any_kept = summed > 0.0
        safe = jnp.where(any_kept, summed, 1.0)
        rows = (acc * jnp.where(any_kept, 1.0 / safe, 0.0)).astype(jnp.bfloat16)
        lse = jnp.where(any_kept, top + jnp.log2(safe), NEGATIVE)
        stat = jnp.zeros((nodes, LANES), jnp.float32)
        for h in range(heads):
            span = slice(h * nodes, (h + 1) * nodes)
            projected = jnp.dot(
                rows[span], w[origin * heads + h], preferred_element_type=jnp.float32
            )
            dst[:, h * dim_v : (h + 1) * dim_v] = projected.astype(jnp.bfloat16)
            stat = jnp.where(lane % heads == h, lse[span], stat)
        high = stat.astype(jnp.bfloat16)
        rest = stat - high.astype(jnp.float32)
        middle = rest.astype(jnp.bfloat16)
        low = (rest - middle.astype(jnp.float32)).astype(jnp.bfloat16)
        packed = jnp.where(
            lane < heads,
            high.astype(jnp.float32),
            jnp.where(lane < 2 * heads, middle.astype(jnp.float32), low.astype(jnp.float32)),
        )
        dst[:, width : width + LANES] = packed.astype(jnp.bfloat16)

    w_copy().wait()

    @pl.loop(0, requests)
    def _(r):
        for copy in load_copies(r):
            copy.wait()
        q = qbuf[me, r].T
        keys = tree_ref[...].reshape(total, tree_ref.shape[2])
        s = lax.dot_general(q, keys, (((1,), (1,)), ((), ())), preferred_element_type=jnp.float32)
        seen = jnp.concatenate([reach[r]] * heads, axis=0) > 0.5
        s = jnp.where(seen, s * scale, NEGATIVE)
        top, summed, acc = stats(s, keys[:, :dim_lat])
        finish(top, summed, acc, me, parts.at[me, r])

    flipped = jnp.where(2 * me < n, 1, 0)

    def place(u, first, count):
        t = jnp.maximum(u - count, 0)
        own = u < count
        d = t // (2 * count) + 1
        side = lax.rem(t // count + flipped, 2)
        r = first + lax.rem(u, count)
        origin = jnp.where(own, me, me - d + 2 * d * side)
        valid = jnp.logical_and(origin >= 0, origin < n)
        if first:
            valid = jnp.logical_and(valid, jnp.logical_or(own, jnp.logical_not(at_end)))
        return origin, r, side, jnp.logical_not(own), valid

    classes = [(0, kept)] + ([(kept, moved)] if moved else [])

    def events(first, u):
        if not moved:
            return
        if first:

            @pl.when(jnp.logical_and(near_end, u == 0))
            def _():
                for stage in range(2, len(stages) + 1):
                    for g in range(moved):
                        share_stage(g, stage)
                if len(stages) == 1:
                    for g in range(moved):
                        share_stage(g, 1)

            return

        @pl.when(jnp.logical_and(near_end, u == kept + 1))
        def _():
            share_stage(0, 0)

        @pl.when(jnp.logical_and(near_end, u == 2 * kept))
        def _():
            for g in range(1, moved):
                share_stage(g, 0)
            if len(stages) > 1:
                share_stage(0, 1)

        @pl.when(jnp.logical_and(near_end, u == 3 * kept))
        def _():
            if len(stages) > 1:
                for g in range(1, moved):
                    share_stage(g, 1)

    for first, count in classes:

        @pl.loop(0, count * (2 * n - 1))
        def _(u):
            origin, r, side, foreign, valid = place(u, first, count)
            events(first, u)

            @pl.when(jnp.logical_and(foreign, valid))
            def _():
                hop_copy(origin, r, side).wait_recv()

                @pl.when(sends_on(r, side))
                def _():
                    hop_copy(origin, r, side).start()

            @pl.when(valid)
            def _():
                q = qbuf[origin, r].T
                top, summed, acc = stats(page_scores(q, r, r, me), lat[r])
                if first:
                    top_ref[...] = top
                    sum_ref[...] = summed
                    acc_ref[...] = acc

                    @pl.when(jnp.logical_and(near_end, origin != end_side))
                    def _():
                        extra = r + moved
                        top_x, sum_x, acc_x = stats(page_scores(q, extra, r, end_side), lat[extra])
                        top_a = top_ref[...]
                        both = jnp.maximum(top_a, top_x)
                        f_a, f_x = jnp.exp2(top_a - both), jnp.exp2(top_x - both)
                        top_ref[...] = both
                        sum_ref[...] = sum_ref[...] * f_a + sum_x * f_x
                        acc_ref[...] = acc_ref[...] * f_a + acc_x * f_x

                    top, summed, acc = top_ref[...], sum_ref[...], acc_ref[...]

                finish(top, summed, acc, origin, mine.at[origin, r])

                @pl.when(foreign)
                def _():
                    part_copy(origin, r, me).start()

    def arrives(r, holder):
        if not moved:
            return None
        last = jnp.logical_or(holder == 0, holder == n - 1)
        return jnp.logical_not(jnp.logical_and(last, r >= kept))

    eye = lax.broadcasted_iota(jnp.int32, (nodes, nodes), 0) == lax.broadcasted_iota(
        jnp.int32, (nodes, nodes), 1
    )

    @pl.loop(0, requests)
    def _(r):
        @pl.loop(1, n)
        def _(k):
            holder = lax.rem(me + k, n)
            if moved:

                @pl.when(arrives(r, holder))
                def _():
                    part_copy(me, r, holder).wait_recv()

            else:
                part_copy(me, r, holder).wait_recv()

        def lse_of(stat):
            stat = stat.astype(jnp.float32)
            lse = stat + pltpu.roll(stat, LANES - heads, 1) + pltpu.roll(stat, LANES - 2 * heads, 1)
            return jnp.where(lane < heads, lse, NEGATIVE)

        own = mine[me, r]
        own_lse = lse_of(own[:, width:])
        top = lax.fori_loop(
            0,
            n,
            lambda k, best: jnp.maximum(best, lse_of(parts[k, r, :, width : width + LANES])),
            own_lse,
            unroll=n <= 8,
        )
        top = jnp.where(lane < heads, top, 0.0)

        def add(carried, lse, part):
            weight_sum, summed = carried
            weight = jnp.exp2(lse - top)
            spread = jnp.concatenate(
                [jnp.broadcast_to(weight[:, h : h + 1], (nodes, dim_v)) for h in range(heads)], axis=1
            )
            return weight_sum + spread, summed + spread * part.astype(jnp.float32)

        zero = jnp.zeros((nodes, width), jnp.float32)
        weight_sum, summed = lax.fori_loop(
            0,
            n,
            lambda k, carried: add(
                carried, lse_of(parts[k, r, :, width : width + LANES]), parts[k, r, :, :width]
            ),
            add((zero, zero), own_lse, own[:, :width]),
            unroll=n <= 8,
        )
        alive = alive_ref[pl.ds(r, 1), :].astype(jnp.float32)
        alive = jnp.sum(jnp.where(eye, alive, 0.0), axis=1, keepdims=True)
        out_ref[r] = (summed / weight_sum * alive).astype(out_ref.dtype)

    if moved:

        @pl.when(at_end)
        def _():
            @pl.loop(0, moved)
            def _(g):
                for copy in page_copies(g):
                    copy.wait_send()

        @pl.when(near_end)
        def _():
            @pl.loop(0, moved)
            def _(g):
                for stage in range(len(stages)):
                    for copy in share_copies(g, stage):
                        copy.wait_send()

    @pl.loop(0, requests)
    def _(r):
        for side in (0, 1):

            @pl.when(sends_on(r, side))
            def _():
                own_copy(r, side).wait_send()

    for first, count in classes:

        @pl.loop(0, count * (2 * n - 1))
        def _(u):
            origin, r, side, foreign, valid = place(u, first, count)

            @pl.when(jnp.logical_and(foreign, valid))
            def _():
                @pl.when(sends_on(r, side))
                def _():
                    hop_copy(origin, r, side).wait_send()

                part_copy(origin, r, me).wait_send()


def shards(
    queries,
    tree_keys,
    parents,
    node_live,
    lengths,
    start_device,
    cache_latent,
    cache_rope,
    up_weight,
):
    n = lax.axis_size("blk")
    requests, dim_q, cols = queries.shape
    nodes = tree_keys.shape[1]
    _, page, dim_lat = cache_latent.shape
    dim_rope = cache_rope.shape[1]
    dim_v = up_weight.shape[2]
    width = cols // nodes * dim_v
    bf16 = jnp.bfloat16
    scale = math.log2(math.e) / math.sqrt(DN + dim_rope)
    peers = lax.axis_size("head")
    movable = n >= 4 and peers & (peers - 1) == 0 < peers - 1 and page % (peers * LANES) == 0
    moved = requests // 2 if movable else 0
    slots = max(moved, 1)
    vmem = pl.BlockSpec(memory_space=pltpu.VMEM)
    smem = pl.BlockSpec(memory_space=pltpu.SMEM)
    anywhere = pl.BlockSpec(memory_space=pl.ANY)
    return pl.pallas_call(
        functools.partial(kernel, n, peers, moved, scale),
        out_shape=jax.ShapeDtypeStruct((requests, nodes, width), bf16),
        in_specs=[anywhere, vmem, vmem, vmem, smem, smem, anywhere, anywhere, anywhere],
        out_specs=vmem,
        scratch_shapes=[
            pltpu.VMEM((n, requests, dim_q, cols), bf16),
            pltpu.VMEM((requests + moved, page, dim_lat), bf16),
            pltpu.VMEM((requests + moved, dim_rope, page), bf16),
            pltpu.VMEM(up_weight.shape, bf16),
            pltpu.VMEM((n, requests, nodes, width + LANES), bf16),
            pltpu.VMEM((n, requests, nodes, width + LANES), bf16),
            pltpu.VMEM((requests, nodes, requests * nodes), jnp.float32),
            pltpu.VMEM((cols, 1), jnp.float32),
            pltpu.VMEM((cols, 1), jnp.float32),
            pltpu.VMEM((cols, dim_lat), jnp.float32),
            pltpu.SemaphoreType.DMA((3, requests)),
            pltpu.SemaphoreType.DMA,
            pltpu.SemaphoreType.DMA((2, n, requests)),
            pltpu.SemaphoreType.DMA((n, requests)),
            pltpu.SemaphoreType.DMA((n, requests)),
            pltpu.SemaphoreType.DMA((n, requests)),
            pltpu.SemaphoreType.DMA((2, slots)),
            pltpu.SemaphoreType.DMA((2, slots, peers)),
            pltpu.SemaphoreType.DMA((2, slots, peers)),
        ],
        compiler_params=pltpu.CompilerParams(
            collective_id=0, has_side_effects=True, vmem_limit_bytes=60 * 1024 * 1024
        ),
        name="tree_attention",
    )(
        queries,
        tree_keys,
        parents,
        node_live,
        lengths,
        start_device,
        cache_latent,
        cache_rope,
        up_weight,
    )


def solution(mesh):
    return jax.shard_map(
        shards,
        mesh=mesh,
        in_specs=(
            P("grp", None, ("head", "blk")),
            P("grp", None, None),
            P("grp", None),
            P("grp", None),
            P("grp"),
            P("grp"),
            P("grp", "blk", None),
            P("grp", None, "blk"),
            P("head", None, None),
        ),
        out_specs=P("grp", None, ("head", "blk")),
        check_vma=False,
    )
```

```python
import functools
import math

import jax
import jax.numpy as jnp
from jax import lax
from jax.experimental import pallas as pl
from jax.experimental.pallas import tpu as pltpu
from jax.sharding import PartitionSpec as P

DN = 128
NEGATIVE = -1e30
FLOOR = -1e29
LANES = 128


def kernel(
    n,
    peers,
    moved,
    scale,
    q_hbm,
    tree_ref,
    parent_ref,
    alive_ref,
    length_ref,
    first_ref,
    lat_hbm,
    rope_hbm,
    w_hbm,
    out_ref,
    qbuf,
    keyed,
    rope,
    valued,
    w,
    parts,
    mine,
    reach,
    top_ref,
    sum_ref,
    acc_ref,
    load_sem,
    w_sem,
    q_send,
    q_recv,
    p_send,
    p_recv,
    page_send,
    peer_send,
    page_recv,
):
    me = lax.axis_index("blk")
    lane_me = lax.axis_index("head")
    requests, dim_q, cols = q_hbm.shape
    nodes = tree_ref.shape[1]
    page, dim_lat = lat_hbm.shape[1:]
    dim_pad = keyed.shape[2]
    dim_v = w.shape[2]
    heads = cols // nodes
    width = heads * dim_v
    kept = requests - moved
    share = page // peers
    mesh_id = pl.DeviceIdType.MESH
    at_end = jnp.logical_or(me == 0, me == n - 1)
    near_end = jnp.logical_or(me == 1, me == n - 2)
    end_side = jnp.where(me <= 1, 0, n - 1)

    def chunk(origin, r):
        return qbuf.at[origin, r, :dim_q]

    def load_copies(r):
        return (
            pltpu.make_async_copy(q_hbm.at[r], chunk(me, r), load_sem.at[0, r]),
            pltpu.make_async_copy(lat_hbm.at[r], keyed.at[r, :, :dim_lat], load_sem.at[1, r]),
            pltpu.make_async_copy(rope_hbm.at[r], rope.at[r], load_sem.at[2, r]),
        )

    def w_copy():
        return pltpu.make_async_copy(w_hbm, w, w_sem)

    def own_copy(r, side):
        return pltpu.make_async_remote_copy(
            src_ref=q_hbm.at[r],
            dst_ref=chunk(me, r),
            send_sem=q_send.at[side, me, r],
            recv_sem=q_recv.at[me, r],
            device_id={"blk": me + 1 - 2 * side},
            device_id_type=mesh_id,
        )

    def hop_copy(origin, r, side):
        return pltpu.make_async_remote_copy(
            src_ref=chunk(origin, r),
            dst_ref=chunk(origin, r),
            send_sem=q_send.at[side, origin, r],
            recv_sem=q_recv.at[origin, r],
            device_id={"blk": me + 1 - 2 * side},
            device_id_type=mesh_id,
        )

    def part_copy(origin, r, holder):
        return pltpu.make_async_remote_copy(
            src_ref=mine.at[origin, r],
            dst_ref=parts.at[holder, r],
            send_sem=p_send.at[origin, r],
            recv_sem=p_recv.at[holder, r],
            device_id={"blk": origin},
            device_id_type=mesh_id,
        )

    def rows_of(j):
        return pl.ds(pl.multiple_of(j * share, share), share)

    def page_copies(g):
        inner = jnp.where(me == 0, 1, n - 2)
        mine_rows = rows_of(lane_me)
        return (
            pltpu.make_async_remote_copy(
                src_ref=lat_hbm.at[kept + g, mine_rows],
                dst_ref=keyed.at[requests + g, mine_rows, :dim_lat],
                send_sem=page_send.at[0, g],
                recv_sem=page_recv.at[0, g, lane_me],
                device_id={"blk": inner},
                device_id_type=mesh_id,
            ),
            pltpu.make_async_remote_copy(
                src_ref=rope_hbm.at[kept + g, :, mine_rows],
                dst_ref=rope.at[requests + g, :, mine_rows],
                send_sem=page_send.at[1, g],
                recv_sem=page_recv.at[1, g, lane_me],
                device_id={"blk": inner},
                device_id_type=mesh_id,
            ),
        )

    stages = []
    while moved and (peers >> len(stages)) > 1:
        stages.append(peers >> (len(stages) + 1))

    def partner(j, gap):
        return j + gap * (1 - 2 * lax.rem(j // gap, 2))

    def held(stage):
        slices = [lane_me]
        for gap in stages[:stage]:
            slices = slices + [partner(j, gap) for j in slices]
        return slices

    def share_copies(g, stage):
        target = partner(lane_me, stages[stage])
        pieces = held(stage)
        return [
            pltpu.make_async_remote_copy(
                src_ref=view,
                dst_ref=view,
                send_sem=peer_send.at[i, g, len(pieces) - 1 + at],
                recv_sem=page_recv.at[i, g, j],
                device_id={"head": target},
                device_id_type=mesh_id,
            )
            for at, j in enumerate(pieces)
            for i, view in enumerate(
                (keyed.at[requests + g, rows_of(j), :dim_lat], rope.at[requests + g, :, rows_of(j)])
            )
        ]

    def await_pieces(g, pieces):
        for j in pieces:
            for i, view in enumerate(
                (keyed.at[requests + g, rows_of(j), :dim_lat], rope.at[requests + g, :, rows_of(j)])
            ):
                pltpu.make_async_remote_copy(
                    src_ref=view,
                    dst_ref=view,
                    send_sem=page_send.at[i, g],
                    recv_sem=page_recv.at[i, g, j],
                    device_id={"blk": me},
                    device_id_type=mesh_id,
                ).wait_recv()

    def share_stage(g, stage):
        pieces = held(stage)
        await_pieces(g, pieces[len(pieces) // 2 :])
        if stage < len(stages):
            for copy in share_copies(g, stage):
                copy.start()

    barrier = pltpu.get_barrier_semaphore()

    @pl.loop(1, n)
    def _(k):
        pl.semaphore_signal(
            barrier, inc=1, device_id={"blk": lax.rem(me + k, n)}, device_id_type=mesh_id
        )

    if moved:

        @pl.loop(1, peers)
        def _(k):
            pl.semaphore_signal(
                barrier,
                inc=1,
                device_id={"head": lax.rem(lane_me + k, peers)},
                device_id_type=mesh_id,
            )

    @pl.loop(0, requests)
    def _(r):
        for copy in load_copies(r):
            copy.start()

    w_copy().start()
    pl.semaphore_wait(barrier, n - 1 + (peers - 1 if moved else 0))

    def sends_on(r, side):
        ahead = me + 1 - 2 * side
        valid = jnp.logical_and(ahead >= 0, ahead < n)
        if moved:
            last = jnp.logical_or(ahead == 0, ahead == n - 1)
            valid = jnp.logical_and(valid, jnp.logical_not(jnp.logical_and(last, r >= kept)))
        return valid

    if moved:

        @pl.when(at_end)
        def _():
            @pl.loop(0, moved)
            def _(g):
                for copy in page_copies(g):
                    copy.start()

    @pl.loop(0, requests)
    def _(r):
        for side in (0, 1):

            @pl.when(sends_on(r, side))
            def _():
                own_copy(r, side).start()

    lane = lax.broadcasted_iota(jnp.int32, (nodes, LANES), 1)
    total = requests * nodes
    column = lax.broadcasted_iota(jnp.int32, (total, total), 1)
    row = lax.broadcasted_iota(jnp.int32, (total, total), 0)
    parent = jnp.concatenate(
        [parent_ref[r : r + 1, :] + r * nodes for r in range(requests)], axis=1
    )
    reached = jnp.where(jnp.logical_or(parent == row, row == column), 1.0, 0.0)
    for _ in range(max(nodes - 1, 1).bit_length()):
        factor = reached.astype(jnp.bfloat16)
        reached = jnp.minimum(jnp.dot(factor, factor, preferred_element_type=jnp.float32), 1.0)
    reach[...] = reached.astype(jnp.bfloat16)

    @pl.loop(0, n)
    def _(origin):
        @pl.loop(0, requests)
        def _(r):
            pad = lax.broadcasted_iota(jnp.int32, (dim_pad - dim_q, cols), 0)
            qbuf[origin, r, dim_q:] = jnp.where(pad == 0, 1.0, 0.0).astype(jnp.bfloat16)

    if moved:
        for end in (0, n - 1):

            @pl.when(me != end)
            def _():
                @pl.loop(0, moved)
                def _(g):
                    blank = parts.at[end, kept + g]
                    blank[:, :width] = jnp.zeros((nodes, width), jnp.bfloat16)
                    blank[:, width:] = jnp.where(lane < heads, NEGATIVE, 0.0).astype(jnp.bfloat16)

    def prepare(place, r, holder):
        turn = lax.rem(holder - first_ref[r] + n, n)
        live = length_ref[r] - turn * page
        shape = (page, dim_pad - dim_q)
        slot = lax.broadcasted_iota(jnp.int32, shape, 0)
        pad = lax.broadcasted_iota(jnp.int32, shape, 1)
        hide = jnp.where(jnp.logical_and(pad == 0, slot >= live), NEGATIVE, 0.0)
        keyed[place, :, dim_lat:] = jnp.concatenate(
            [rope[place].T, hide.astype(jnp.bfloat16)], axis=1
        )
        valued[place] = keyed[place, :, :dim_lat].T

    def stats(scores, values):
        top = jnp.maximum(jnp.max(scores, axis=0, keepdims=True), FLOOR)
        weights = jnp.exp2((scores - top) * scale)
        summed = jnp.sum(weights, axis=0, keepdims=True)
        acc = jnp.dot(values, weights.astype(jnp.bfloat16), preferred_element_type=jnp.float32)
        return top, summed, acc

    def page_stats(place, q):
        return stats(jnp.dot(keyed[place], q, preferred_element_type=jnp.float32), valued[place])

    def finish(top, summed, acc, origin, dst):
        any_kept = summed > 0.0
        safe = jnp.where(any_kept, summed, 1.0)
        rows = (acc * jnp.where(any_kept, 1.0 / safe, 0.0)).astype(jnp.bfloat16).T
        lse = jnp.where(any_kept, top * scale + jnp.log2(safe), NEGATIVE)
        lse = jnp.broadcast_to(lse, (LANES, cols)).T
        stat = jnp.zeros((nodes, LANES), jnp.float32)
        for h in range(heads):
            span = slice(h * nodes, (h + 1) * nodes)
            projected = jnp.dot(
                rows[span], w[origin * heads + h], preferred_element_type=jnp.float32
            )
            dst[:, h * dim_v : (h + 1) * dim_v] = projected.astype(jnp.bfloat16)
            stat = jnp.where(lane % heads == h, lse[span], stat)
        high = stat.astype(jnp.bfloat16)
        rest = stat - high.astype(jnp.float32)
        middle = rest.astype(jnp.bfloat16)
        low = (rest - middle.astype(jnp.float32)).astype(jnp.bfloat16)
        packed = jnp.where(
            lane < heads,
            high.astype(jnp.float32),
            jnp.where(lane < 2 * heads, middle.astype(jnp.float32), low.astype(jnp.float32)),
        )
        dst[:, width : width + LANES] = packed.astype(jnp.bfloat16)

    w_copy().wait()

    @pl.loop(0, requests)
    def _(r):
        for copy in load_copies(r):
            copy.wait()
        prepare(r, r, me)
        q = qbuf[me, r, :dim_q]
        keys = tree_ref[...].reshape(total, dim_q)
        s = jnp.dot(keys, q, preferred_element_type=jnp.float32)
        node = r * nodes + lax.rem(lax.broadcasted_iota(jnp.int32, (total, cols), 1), nodes)
        spread = jnp.where(lax.broadcasted_iota(jnp.int32, (total, cols), 0) == node, 1.0, 0.0)
        seen = jnp.dot(reach[...], spread.astype(jnp.bfloat16), preferred_element_type=jnp.float32)
        s = jnp.where(seen > 0.5, s, NEGATIVE)
        top, summed, acc = stats(s, keys[:, :dim_lat].T)
        finish(top, summed, acc, me, parts.at[me, r])

    flipped = jnp.where(2 * me < n, 1, 0)

    def place(u, first, count):
        t = jnp.maximum(u - count, 0)
        own = u < count
        d = t // (2 * count) + 1
        side = lax.rem(t // count + flipped, 2)
        r = first + lax.rem(u, count)
        origin = jnp.where(own, me, me - d + 2 * d * side)
        valid = jnp.logical_and(origin >= 0, origin < n)
        if first:
            valid = jnp.logical_and(valid, jnp.logical_or(own, jnp.logical_not(at_end)))
        return origin, r, side, jnp.logical_not(own), valid

    classes = [(0, kept)] + ([(kept, moved)] if moved else [])

    def events(first, u):
        if not moved:
            return
        if first:

            @pl.when(jnp.logical_and(near_end, u == 0))
            def _():
                for stage in range(2, len(stages) + 1):
                    for g in range(moved):
                        share_stage(g, stage)
                if len(stages) == 1:
                    for g in range(moved):
                        share_stage(g, 1)

                @pl.loop(0, moved)
                def _(g):
                    prepare(requests + g, kept + g, end_side)

            return

        @pl.when(jnp.logical_and(near_end, u == kept + 1))
        def _():
            share_stage(0, 0)

        @pl.when(jnp.logical_and(near_end, u == 2 * kept))
        def _():
            for g in range(1, moved):
                share_stage(g, 0)
            if len(stages) > 1:
                share_stage(0, 1)

        @pl.when(jnp.logical_and(near_end, u == 3 * kept))
        def _():
            if len(stages) > 1:
                for g in range(1, moved):
                    share_stage(g, 1)

    for first, count in classes:

        @pl.loop(0, count * (2 * n - 1))
        def _(u):
            origin, r, side, foreign, valid = place(u, first, count)
            events(first, u)

            @pl.when(jnp.logical_and(foreign, valid))
            def _():
                hop_copy(origin, r, side).wait_recv()

                @pl.when(sends_on(r, side))
                def _():
                    hop_copy(origin, r, side).start()

            @pl.when(valid)
            def _():
                top, summed, acc = page_stats(r, qbuf[origin, r])
                if first:
                    top_ref[...] = top
                    sum_ref[...] = summed
                    acc_ref[...] = acc

                    @pl.when(jnp.logical_and(near_end, origin != end_side))
                    def _():
                        top_x, sum_x, acc_x = page_stats(r + moved, qbuf[origin, r])
                        top_a = top_ref[...]
                        both = jnp.maximum(top_a, top_x)
                        f_a = jnp.exp2((top_a - both) * scale)
                        f_x = jnp.exp2((top_x - both) * scale)
                        top_ref[...] = both
                        sum_ref[...] = sum_ref[...] * f_a + sum_x * f_x
                        acc_ref[...] = acc_ref[...] * f_a + acc_x * f_x

                    top, summed, acc = top_ref[...], sum_ref[...], acc_ref[...]

                finish(top, summed, acc, origin, mine.at[origin, r])

                @pl.when(foreign)
                def _():
                    part_copy(origin, r, me).start()

    def arrives(r, holder):
        if not moved:
            return None
        last = jnp.logical_or(holder == 0, holder == n - 1)
        return jnp.logical_not(jnp.logical_and(last, r >= kept))

    eye = lax.broadcasted_iota(jnp.int32, (nodes, nodes), 0) == lax.broadcasted_iota(
        jnp.int32, (nodes, nodes), 1
    )

    @pl.loop(0, requests)
    def _(r):
        @pl.loop(1, n)
        def _(k):
            holder = lax.rem(me + k, n)
            if moved:

                @pl.when(arrives(r, holder))
                def _():
                    part_copy(me, r, holder).wait_recv()

            else:
                part_copy(me, r, holder).wait_recv()

        def lse_of(stat):
            stat = stat.astype(jnp.float32)
            lse = stat + pltpu.roll(stat, LANES - heads, 1) + pltpu.roll(stat, LANES - 2 * heads, 1)
            return jnp.where(lane < heads, lse, NEGATIVE)

        own = mine[me, r]
        own_lse = lse_of(own[:, width:])
        top = lax.fori_loop(
            0,
            n,
            lambda k, best: jnp.maximum(best, lse_of(parts[k, r, :, width : width + LANES])),
            own_lse,
            unroll=n <= 8,
        )
        top = jnp.where(lane < heads, top, 0.0)

        def add(carried, lse, part):
            weight_sum, summed = carried
            weight = jnp.exp2(lse - top)
            spread = jnp.concatenate(
                [jnp.broadcast_to(weight[:, h : h + 1], (nodes, dim_v)) for h in range(heads)], axis=1
            )
            return weight_sum + spread, summed + spread * part.astype(jnp.float32)

        zero = jnp.zeros((nodes, width), jnp.float32)
        weight_sum, summed = lax.fori_loop(
            0,
            n,
            lambda k, carried: add(
                carried, lse_of(parts[k, r, :, width : width + LANES]), parts[k, r, :, :width]
            ),
            add((zero, zero), own_lse, own[:, :width]),
            unroll=n <= 8,
        )
        alive = alive_ref[pl.ds(r, 1), :].astype(jnp.float32)
        alive = jnp.sum(jnp.where(eye, alive, 0.0), axis=1, keepdims=True)
        out_ref[r] = (summed / weight_sum * alive).astype(out_ref.dtype)

    if moved:

        @pl.when(at_end)
        def _():
            @pl.loop(0, moved)
            def _(g):
                for copy in page_copies(g):
                    copy.wait_send()

        @pl.when(near_end)
        def _():
            @pl.loop(0, moved)
            def _(g):
                for stage in range(len(stages)):
                    for copy in share_copies(g, stage):
                        copy.wait_send()

    @pl.loop(0, requests)
    def _(r):
        for side in (0, 1):

            @pl.when(sends_on(r, side))
            def _():
                own_copy(r, side).wait_send()

    for first, count in classes:

        @pl.loop(0, count * (2 * n - 1))
        def _(u):
            origin, r, side, foreign, valid = place(u, first, count)

            @pl.when(jnp.logical_and(foreign, valid))
            def _():
                @pl.when(sends_on(r, side))
                def _():
                    hop_copy(origin, r, side).wait_send()

                part_copy(origin, r, me).wait_send()


def shards(
    queries,
    tree_keys,
    parents,
    node_live,
    lengths,
    start_device,
    cache_latent,
    cache_rope,
    up_weight,
):
    n = lax.axis_size("blk")
    requests, dim_q, cols = queries.shape
    nodes = tree_keys.shape[1]
    _, page, dim_lat = cache_latent.shape
    dim_rope = cache_rope.shape[1]
    dim_v = up_weight.shape[2]
    width = cols // nodes * dim_v
    bf16 = jnp.bfloat16
    scale = math.log2(math.e) / math.sqrt(DN + dim_rope)
    dim_pad = (dim_q // LANES + 1) * LANES
    peers = lax.axis_size("head")
    movable = n >= 4 and peers & (peers - 1) == 0 < peers - 1 and page % (peers * LANES) == 0
    moved = requests // 2 if movable else 0
    slots = max(moved, 1)
    vmem = pl.BlockSpec(memory_space=pltpu.VMEM)
    smem = pl.BlockSpec(memory_space=pltpu.SMEM)
    anywhere = pl.BlockSpec(memory_space=pl.ANY)
    return pl.pallas_call(
        functools.partial(kernel, n, peers, moved, scale),
        out_shape=jax.ShapeDtypeStruct((requests, nodes, width), bf16),
        in_specs=[anywhere, vmem, vmem, vmem, smem, smem, anywhere, anywhere, anywhere],
        out_specs=vmem,
        scratch_shapes=[
            pltpu.VMEM((n, requests, dim_pad, cols), bf16),
            pltpu.VMEM((requests + moved, page, dim_pad), bf16),
            pltpu.VMEM((requests + moved, dim_rope, page), bf16),
            pltpu.VMEM((requests + moved, dim_lat, page), bf16),
            pltpu.VMEM(up_weight.shape, bf16),
            pltpu.VMEM((n, requests, nodes, width + LANES), bf16),
            pltpu.VMEM((n, requests, nodes, width + LANES), bf16),
            pltpu.VMEM((requests * nodes, requests * nodes), bf16),
            pltpu.VMEM((1, cols), jnp.float32),
            pltpu.VMEM((1, cols), jnp.float32),
            pltpu.VMEM((dim_lat, cols), jnp.float32),
            pltpu.SemaphoreType.DMA((3, requests)),
            pltpu.SemaphoreType.DMA,
            pltpu.SemaphoreType.DMA((2, n, requests)),
            pltpu.SemaphoreType.DMA((n, requests)),
            pltpu.SemaphoreType.DMA((n, requests)),
            pltpu.SemaphoreType.DMA((n, requests)),
            pltpu.SemaphoreType.DMA((2, slots)),
            pltpu.SemaphoreType.DMA((2, slots, peers)),
            pltpu.SemaphoreType.DMA((2, slots, peers)),
        ],
        compiler_params=pltpu.CompilerParams(
            collective_id=0, has_side_effects=True, vmem_limit_bytes=60 * 1024 * 1024
        ),
        name="tree_attention",
    )(
        queries,
        tree_keys,
        parents,
        node_live,
        lengths,
        start_device,
        cache_latent,
        cache_rope,
        up_weight,
    )


def solution(mesh):
    return jax.shard_map(
        shards,
        mesh=mesh,
        in_specs=(
            P("grp", None, ("head", "blk")),
            P("grp", None, None),
            P("grp", None),
            P("grp", None),
            P("grp"),
            P("grp"),
            P("grp", "blk", None),
            P("grp", None, "blk"),
            P("head", None, None),
        ),
        out_specs=P("grp", None, ("head", "blk")),
        check_vma=False,
    )
```

```python
import functools
import math

import jax
import jax.numpy as jnp
from jax import lax
from jax.experimental import pallas as pl
from jax.experimental.pallas import tpu as pltpu
from jax.sharding import PartitionSpec as P

DN = 128
NEGATIVE = -1e30
FLOOR = -1e29
LANES = 128


def kernel(
    n,
    peers,
    moved,
    scale,
    q_hbm,
    tree_ref,
    parent_ref,
    alive_ref,
    length_ref,
    first_ref,
    lat_hbm,
    rope_hbm,
    w_hbm,
    out_ref,
    qbuf,
    lat,
    rope,
    w,
    parts,
    mine,
    reach,
    top_ref,
    sum_ref,
    acc_ref,
    load_sem,
    w_sem,
    q_send,
    q_recv,
    p_send,
    p_recv,
    page_send,
    peer_send,
    page_recv,
):
    me = lax.axis_index("blk")
    lane_me = lax.axis_index("head")
    requests, _, cols = q_hbm.shape
    nodes = tree_ref.shape[1]
    dim_lat = lat.shape[2]
    page = lat.shape[1]
    dim_v = w.shape[2]
    heads = cols // nodes
    width = heads * dim_v
    kept = requests - moved
    share = page // peers
    mesh_id = pl.DeviceIdType.MESH
    at_end = jnp.logical_or(me == 0, me == n - 1)
    near_end = jnp.logical_or(me == 1, me == n - 2)
    end_side = jnp.where(me <= 1, 0, n - 1)

    def load_copies(r):
        return (
            pltpu.make_async_copy(q_hbm.at[r], qbuf.at[me, r], load_sem.at[0, r]),
            pltpu.make_async_copy(lat_hbm.at[r], lat.at[r], load_sem.at[1, r]),
            pltpu.make_async_copy(rope_hbm.at[r], rope.at[r], load_sem.at[2, r]),
        )

    def w_copy():
        return pltpu.make_async_copy(w_hbm, w, w_sem)

    def own_copy(r, side):
        return pltpu.make_async_remote_copy(
            src_ref=q_hbm.at[r],
            dst_ref=qbuf.at[me, r],
            send_sem=q_send.at[side, me, r],
            recv_sem=q_recv.at[me, r],
            device_id={"blk": me + 1 - 2 * side},
            device_id_type=mesh_id,
        )

    def hop_copy(origin, r, side):
        return pltpu.make_async_remote_copy(
            src_ref=qbuf.at[origin, r],
            dst_ref=qbuf.at[origin, r],
            send_sem=q_send.at[side, origin, r],
            recv_sem=q_recv.at[origin, r],
            device_id={"blk": me + 1 - 2 * side},
            device_id_type=mesh_id,
        )

    def part_copy(origin, r, holder):
        return pltpu.make_async_remote_copy(
            src_ref=mine.at[origin, r],
            dst_ref=parts.at[holder, r],
            send_sem=p_send.at[origin, r],
            recv_sem=p_recv.at[holder, r],
            device_id={"blk": origin},
            device_id_type=mesh_id,
        )

    def rows_of(j):
        return pl.ds(pl.multiple_of(j * share, share), share)

    def page_copies(g):
        inner = jnp.where(me == 0, 1, n - 2)
        mine_rows = rows_of(lane_me)
        return (
            pltpu.make_async_remote_copy(
                src_ref=lat_hbm.at[kept + g, mine_rows],
                dst_ref=lat.at[requests + g, mine_rows],
                send_sem=page_send.at[0, g],
                recv_sem=page_recv.at[0, g, lane_me],
                device_id={"blk": inner},
                device_id_type=mesh_id,
            ),
            pltpu.make_async_remote_copy(
                src_ref=rope_hbm.at[kept + g, :, mine_rows],
                dst_ref=rope.at[requests + g, :, mine_rows],
                send_sem=page_send.at[1, g],
                recv_sem=page_recv.at[1, g, lane_me],
                device_id={"blk": inner},
                device_id_type=mesh_id,
            ),
        )

    stages = []
    while moved and (peers >> len(stages)) > 1:
        stages.append(peers >> (len(stages) + 1))

    def partner(j, gap):
        return j + gap * (1 - 2 * lax.rem(j // gap, 2))

    def held(stage):
        slices = [lane_me]
        for gap in stages[:stage]:
            slices = slices + [partner(j, gap) for j in slices]
        return slices

    def share_copies(g, stage):
        target = partner(lane_me, stages[stage])
        pieces = held(stage)
        return [
            pltpu.make_async_remote_copy(
                src_ref=view,
                dst_ref=view,
                send_sem=peer_send.at[i, g, len(pieces) - 1 + at],
                recv_sem=page_recv.at[i, g, j],
                device_id={"head": target},
                device_id_type=mesh_id,
            )
            for at, j in enumerate(pieces)
            for i, view in enumerate(
                (lat.at[requests + g, rows_of(j)], rope.at[requests + g, :, rows_of(j)])
            )
        ]

    def await_pieces(g, pieces):
        for j in pieces:
            for i, view in enumerate(
                (lat.at[requests + g, rows_of(j)], rope.at[requests + g, :, rows_of(j)])
            ):
                pltpu.make_async_remote_copy(
                    src_ref=view,
                    dst_ref=view,
                    send_sem=page_send.at[i, g],
                    recv_sem=page_recv.at[i, g, j],
                    device_id={"blk": me},
                    device_id_type=mesh_id,
                ).wait_recv()

    def share_stage(g, stage):
        pieces = held(stage)
        await_pieces(g, pieces[len(pieces) // 2 :])
        if stage < len(stages):
            for copy in share_copies(g, stage):
                copy.start()

    barrier = pltpu.get_barrier_semaphore()

    @pl.loop(1, n)
    def _(k):
        pl.semaphore_signal(
            barrier, inc=1, device_id={"blk": lax.rem(me + k, n)}, device_id_type=mesh_id
        )

    if moved:

        @pl.loop(1, peers)
        def _(k):
            pl.semaphore_signal(
                barrier,
                inc=1,
                device_id={"head": lax.rem(lane_me + k, peers)},
                device_id_type=mesh_id,
            )

    @pl.loop(0, requests)
    def _(r):
        for copy in load_copies(r):
            copy.start()

    w_copy().start()
    pl.semaphore_wait(barrier, n - 1 + (peers - 1 if moved else 0))

    def sends_on(r, side):
        ahead = me + 1 - 2 * side
        valid = jnp.logical_and(ahead >= 0, ahead < n)
        if moved:
            last = jnp.logical_or(ahead == 0, ahead == n - 1)
            valid = jnp.logical_and(valid, jnp.logical_not(jnp.logical_and(last, r >= kept)))
        return valid

    if moved:

        @pl.when(at_end)
        def _():
            @pl.loop(0, moved)
            def _(g):
                for copy in page_copies(g):
                    copy.start()

    def send_own():
        @pl.loop(0, requests)
        def _(r):
            for side in (0, 1):

                @pl.when(sends_on(r, side))
                def _():
                    own_copy(r, side).start()

    @pl.when(jnp.logical_not(at_end) if moved else me >= 0)
    def _():
        send_own()

    lane = lax.broadcasted_iota(jnp.int32, (nodes, LANES), 1)
    total = requests * nodes
    column = lax.broadcasted_iota(jnp.int32, (total, total), 1)
    row = lax.broadcasted_iota(jnp.int32, (total, total), 0)
    parent = jnp.concatenate(
        [parent_ref[r : r + 1, :] + r * nodes for r in range(requests)], axis=1
    )
    reached = jnp.where(jnp.logical_or(parent == row, row == column), 1.0, 0.0)
    for _ in range(max(nodes - 1, 1).bit_length()):
        factor = reached.astype(jnp.bfloat16)
        reached = jnp.minimum(jnp.dot(factor, factor, preferred_element_type=jnp.float32), 1.0)
    reach[...] = reached.T.reshape(requests, nodes, total)

    if moved:
        for end in (0, n - 1):

            @pl.when(me != end)
            def _():
                @pl.loop(0, moved)
                def _(g):
                    blank = parts.at[end, kept + g]
                    blank[:, :width] = jnp.zeros((nodes, width), jnp.bfloat16)
                    blank[:, width:] = jnp.where(lane < heads, NEGATIVE, 0.0).astype(jnp.bfloat16)

    def stats(scores, values):
        top = jnp.maximum(jnp.max(scores, axis=1, keepdims=True), FLOOR)
        weights = jnp.exp2(scores - top)
        summed = jnp.sum(weights, axis=1, keepdims=True)
        acc = jnp.dot(weights.astype(jnp.bfloat16), values, preferred_element_type=jnp.float32)
        return top, summed, acc

    def page_scores(q, place, r, holder):
        s = lax.dot_general(
            q[:, :dim_lat], lat[place], (((1,), (1,)), ((), ())), preferred_element_type=jnp.float32
        )
        s = s + jnp.dot(q[:, dim_lat:], rope[place], preferred_element_type=jnp.float32)
        turn = lax.rem(holder - first_ref[r] + n, n)
        live = length_ref[r] - turn * page
        slot = lax.broadcasted_iota(jnp.int32, (1, page), 1)
        return jnp.where(slot < live, s * scale, NEGATIVE)

    def finish(top, summed, acc, origin, dst):
        any_kept = summed > 0.0
        safe = jnp.where(any_kept, summed, 1.0)
        rows = (acc * jnp.where(any_kept, 1.0 / safe, 0.0)).astype(jnp.bfloat16)
        lse = jnp.where(any_kept, top + jnp.log2(safe), NEGATIVE)
        stat = jnp.zeros((nodes, LANES), jnp.float32)
        for h in range(heads):
            span = slice(h * nodes, (h + 1) * nodes)
            projected = jnp.dot(
                rows[span], w[origin * heads + h], preferred_element_type=jnp.float32
            )
            dst[:, h * dim_v : (h + 1) * dim_v] = projected.astype(jnp.bfloat16)
            stat = jnp.where(lane % heads == h, lse[span], stat)
        high = stat.astype(jnp.bfloat16)
        rest = stat - high.astype(jnp.float32)
        middle = rest.astype(jnp.bfloat16)
        low = (rest - middle.astype(jnp.float32)).astype(jnp.bfloat16)
        packed = jnp.where(
            lane < heads,
            high.astype(jnp.float32),
            jnp.where(lane < 2 * heads, middle.astype(jnp.float32), low.astype(jnp.float32)),
        )
        dst[:, width : width + LANES] = packed.astype(jnp.bfloat16)

    w_copy().wait()

    @pl.loop(0, requests)
    def _(r):
        for copy in load_copies(r):
            copy.wait()
        q = qbuf[me, r].T
        keys = tree_ref[...].reshape(total, tree_ref.shape[2])
        s = lax.dot_general(q, keys, (((1,), (1,)), ((), ())), preferred_element_type=jnp.float32)
        seen = jnp.concatenate([reach[r]] * heads, axis=0) > 0.5
        s = jnp.where(seen, s * scale, NEGATIVE)
        top, summed, acc = stats(s, keys[:, :dim_lat])
        finish(top, summed, acc, me, parts.at[me, r])

    flipped = jnp.where(2 * me < n, 1, 0)

    def place(u, first, count):
        t = jnp.maximum(u - count, 0)
        own = u < count
        d = t // (2 * count) + 1
        side = lax.rem(t // count + flipped, 2)
        r = first + lax.rem(u, count)
        origin = jnp.where(own, me, me - d + 2 * d * side)
        valid = jnp.logical_and(origin >= 0, origin < n)
        if first:
            valid = jnp.logical_and(valid, jnp.logical_or(own, jnp.logical_not(at_end)))
        return origin, r, side, jnp.logical_not(own), valid

    classes = [(0, kept)] + ([(kept, moved)] if moved else [])

    def events(first, u):
        if not moved:
            return
        if first:

            @pl.when(jnp.logical_and(near_end, u == 0))
            def _():
                for stage in range(2, len(stages) + 1):
                    for g in range(moved):
                        share_stage(g, stage)
                if len(stages) == 1:
                    for g in range(moved):
                        share_stage(g, 1)

            return

        @pl.when(jnp.logical_and(at_end, u == kept))
        def _():
            @pl.loop(0, moved)
            def _(g):
                for copy in page_copies(g):
                    copy.wait_send()

            send_own()

        @pl.when(jnp.logical_and(near_end, u == kept + 1))
        def _():
            share_stage(0, 0)

        @pl.when(jnp.logical_and(near_end, u == 2 * kept))
        def _():
            for g in range(1, moved):
                share_stage(g, 0)
            if len(stages) > 1:
                share_stage(0, 1)

        @pl.when(jnp.logical_and(near_end, u == 3 * kept))
        def _():
            if len(stages) > 1:
                for g in range(1, moved):
                    share_stage(g, 1)

    for first, count in classes:

        @pl.loop(0, count * (2 * n - 1))
        def _(u):
            origin, r, side, foreign, valid = place(u, first, count)
            events(first, u)

            @pl.when(jnp.logical_and(foreign, valid))
            def _():
                hop_copy(origin, r, side).wait_recv()

                @pl.when(sends_on(r, side))
                def _():
                    hop_copy(origin, r, side).start()

            @pl.when(valid)
            def _():
                q = qbuf[origin, r].T
                top, summed, acc = stats(page_scores(q, r, r, me), lat[r])
                if first:
                    top_ref[...] = top
                    sum_ref[...] = summed
                    acc_ref[...] = acc

                    @pl.when(jnp.logical_and(near_end, origin != end_side))
                    def _():
                        extra = r + moved
                        top_x, sum_x, acc_x = stats(page_scores(q, extra, r, end_side), lat[extra])
                        top_a = top_ref[...]
                        both = jnp.maximum(top_a, top_x)
                        f_a, f_x = jnp.exp2(top_a - both), jnp.exp2(top_x - both)
                        top_ref[...] = both
                        sum_ref[...] = sum_ref[...] * f_a + sum_x * f_x
                        acc_ref[...] = acc_ref[...] * f_a + acc_x * f_x

                    top, summed, acc = top_ref[...], sum_ref[...], acc_ref[...]

                finish(top, summed, acc, origin, mine.at[origin, r])

                @pl.when(foreign)
                def _():
                    part_copy(origin, r, me).start()

    def arrives(r, holder):
        if not moved:
            return None
        last = jnp.logical_or(holder == 0, holder == n - 1)
        return jnp.logical_not(jnp.logical_and(last, r >= kept))

    eye = lax.broadcasted_iota(jnp.int32, (nodes, nodes), 0) == lax.broadcasted_iota(
        jnp.int32, (nodes, nodes), 1
    )

    @pl.loop(0, requests)
    def _(r):
        @pl.loop(1, n)
        def _(k):
            holder = lax.rem(me + k, n)
            if moved:

                @pl.when(arrives(r, holder))
                def _():
                    part_copy(me, r, holder).wait_recv()

            else:
                part_copy(me, r, holder).wait_recv()

        def lse_of(stat):
            stat = stat.astype(jnp.float32)
            lse = stat + pltpu.roll(stat, LANES - heads, 1) + pltpu.roll(stat, LANES - 2 * heads, 1)
            return jnp.where(lane < heads, lse, NEGATIVE)

        own = mine[me, r]
        own_lse = lse_of(own[:, width:])
        top = lax.fori_loop(
            0,
            n,
            lambda k, best: jnp.maximum(best, lse_of(parts[k, r, :, width : width + LANES])),
            own_lse,
            unroll=n <= 8,
        )
        top = jnp.where(lane < heads, top, 0.0)

        def add(carried, lse, part):
            weight_sum, summed = carried
            weight = jnp.exp2(lse - top)
            spread = jnp.concatenate(
                [jnp.broadcast_to(weight[:, h : h + 1], (nodes, dim_v)) for h in range(heads)], axis=1
            )
            return weight_sum + spread, summed + spread * part.astype(jnp.float32)

        zero = jnp.zeros((nodes, width), jnp.float32)
        weight_sum, summed = lax.fori_loop(
            0,
            n,
            lambda k, carried: add(
                carried, lse_of(parts[k, r, :, width : width + LANES]), parts[k, r, :, :width]
            ),
            add((zero, zero), own_lse, own[:, :width]),
            unroll=n <= 8,
        )
        alive = alive_ref[pl.ds(r, 1), :].astype(jnp.float32)
        alive = jnp.sum(jnp.where(eye, alive, 0.0), axis=1, keepdims=True)
        out_ref[r] = (summed / weight_sum * alive).astype(out_ref.dtype)

    if moved:

        @pl.when(near_end)
        def _():
            @pl.loop(0, moved)
            def _(g):
                for stage in range(len(stages)):
                    for copy in share_copies(g, stage):
                        copy.wait_send()

    @pl.loop(0, requests)
    def _(r):
        for side in (0, 1):

            @pl.when(sends_on(r, side))
            def _():
                own_copy(r, side).wait_send()

    for first, count in classes:

        @pl.loop(0, count * (2 * n - 1))
        def _(u):
            origin, r, side, foreign, valid = place(u, first, count)

            @pl.when(jnp.logical_and(foreign, valid))
            def _():
                @pl.when(sends_on(r, side))
                def _():
                    hop_copy(origin, r, side).wait_send()

                part_copy(origin, r, me).wait_send()


def shards(
    queries,
    tree_keys,
    parents,
    node_live,
    lengths,
    start_device,
    cache_latent,
    cache_rope,
    up_weight,
):
    n = lax.axis_size("blk")
    requests, dim_q, cols = queries.shape
    nodes = tree_keys.shape[1]
    _, page, dim_lat = cache_latent.shape
    dim_rope = cache_rope.shape[1]
    dim_v = up_weight.shape[2]
    width = cols // nodes * dim_v
    bf16 = jnp.bfloat16
    scale = math.log2(math.e) / math.sqrt(DN + dim_rope)
    peers = lax.axis_size("head")
    movable = n >= 4 and peers & (peers - 1) == 0 < peers - 1 and page % (peers * LANES) == 0
    moved = requests // 2 if movable else 0
    slots = max(moved, 1)
    vmem = pl.BlockSpec(memory_space=pltpu.VMEM)
    smem = pl.BlockSpec(memory_space=pltpu.SMEM)
    anywhere = pl.BlockSpec(memory_space=pl.ANY)
    return pl.pallas_call(
        functools.partial(kernel, n, peers, moved, scale),
        out_shape=jax.ShapeDtypeStruct((requests, nodes, width), bf16),
        in_specs=[anywhere, vmem, vmem, vmem, smem, smem, anywhere, anywhere, anywhere],
        out_specs=vmem,
        scratch_shapes=[
            pltpu.VMEM((n, requests, dim_q, cols), bf16),
            pltpu.VMEM((requests + moved, page, dim_lat), bf16),
            pltpu.VMEM((requests + moved, dim_rope, page), bf16),
            pltpu.VMEM(up_weight.shape, bf16),
            pltpu.VMEM((n, requests, nodes, width + LANES), bf16),
            pltpu.VMEM((n, requests, nodes, width + LANES), bf16),
            pltpu.VMEM((requests, nodes, requests * nodes), jnp.float32),
            pltpu.VMEM((cols, 1), jnp.float32),
            pltpu.VMEM((cols, 1), jnp.float32),
            pltpu.VMEM((cols, dim_lat), jnp.float32),
            pltpu.SemaphoreType.DMA((3, requests)),
            pltpu.SemaphoreType.DMA,
            pltpu.SemaphoreType.DMA((2, n, requests)),
            pltpu.SemaphoreType.DMA((n, requests)),
            pltpu.SemaphoreType.DMA((n, requests)),
            pltpu.SemaphoreType.DMA((n, requests)),
            pltpu.SemaphoreType.DMA((2, slots)),
            pltpu.SemaphoreType.DMA((2, slots, peers)),
            pltpu.SemaphoreType.DMA((2, slots, peers)),
        ],
        compiler_params=pltpu.CompilerParams(
            collective_id=0, has_side_effects=True, vmem_limit_bytes=60 * 1024 * 1024
        ),
        name="tree_attention",
    )(
        queries,
        tree_keys,
        parents,
        node_live,
        lengths,
        start_device,
        cache_latent,
        cache_rope,
        up_weight,
    )


def solution(mesh):
    return jax.shard_map(
        shards,
        mesh=mesh,
        in_specs=(
            P("grp", None, ("head", "blk")),
            P("grp", None, None),
            P("grp", None),
            P("grp", None),
            P("grp"),
            P("grp"),
            P("grp", "blk", None),
            P("grp", None, "blk"),
            P("head", None, None),
        ),
        out_specs=P("grp", None, ("head", "blk")),
        check_vma=False,
    )
```

```python
import functools
import math

import jax
import jax.numpy as jnp
from jax import lax
from jax.experimental import pallas as pl
from jax.experimental.pallas import tpu as pltpu
from jax.sharding import PartitionSpec as P

DN = 128
NEGATIVE = -1e30
FLOOR = -1e29
LANES = 128


def kernel(
    n,
    peers,
    moved,
    scale,
    q_hbm,
    tree_ref,
    parent_ref,
    alive_ref,
    length_ref,
    first_ref,
    lat_hbm,
    rope_hbm,
    w_hbm,
    out_ref,
    qbuf,
    lat,
    rope,
    w,
    parts,
    mine,
    reach,
    top_ref,
    sum_ref,
    acc_ref,
    load_sem,
    w_sem,
    q_send,
    q_recv,
    p_send,
    p_recv,
    page_send,
    peer_send,
    page_recv,
):
    me = lax.axis_index("blk")
    lane_me = lax.axis_index("head")
    requests, _, cols = q_hbm.shape
    nodes = tree_ref.shape[1]
    dim_lat = lat.shape[2]
    page = lat.shape[1]
    dim_v = w.shape[2]
    heads = cols // nodes
    width = heads * dim_v
    kept = requests - moved
    share = page // peers
    mesh_id = pl.DeviceIdType.MESH
    at_end = jnp.logical_or(me == 0, me == n - 1)
    near_end = jnp.logical_or(me == 1, me == n - 2)
    end_side = jnp.where(me <= 1, 0, n - 1)

    def load_copies(r):
        return (
            pltpu.make_async_copy(q_hbm.at[r], qbuf.at[me, r], load_sem.at[0, r]),
            pltpu.make_async_copy(lat_hbm.at[r], lat.at[r], load_sem.at[1, r]),
            pltpu.make_async_copy(rope_hbm.at[r], rope.at[r], load_sem.at[2, r]),
        )

    def w_copy():
        return pltpu.make_async_copy(w_hbm, w, w_sem)

    def own_copy(r, side):
        return pltpu.make_async_remote_copy(
            src_ref=q_hbm.at[r],
            dst_ref=qbuf.at[me, r],
            send_sem=q_send.at[side, me, r],
            recv_sem=q_recv.at[me, r],
            device_id={"blk": me + 1 - 2 * side},
            device_id_type=mesh_id,
        )

    def hop_copy(origin, r, side):
        return pltpu.make_async_remote_copy(
            src_ref=qbuf.at[origin, r],
            dst_ref=qbuf.at[origin, r],
            send_sem=q_send.at[side, origin, r],
            recv_sem=q_recv.at[origin, r],
            device_id={"blk": me + 1 - 2 * side},
            device_id_type=mesh_id,
        )

    def part_copy(origin, r, holder):
        return pltpu.make_async_remote_copy(
            src_ref=mine.at[origin, r],
            dst_ref=parts.at[holder, r],
            send_sem=p_send.at[origin, r],
            recv_sem=p_recv.at[holder, r],
            device_id={"blk": origin},
            device_id_type=mesh_id,
        )

    def rows_of(j):
        return pl.ds(pl.multiple_of(j * share, share), share)

    def page_copies(g):
        inner = jnp.where(me == 0, 1, n - 2)
        mine_rows = rows_of(lane_me)
        return (
            pltpu.make_async_remote_copy(
                src_ref=lat_hbm.at[kept + g, mine_rows],
                dst_ref=lat.at[requests + g, mine_rows],
                send_sem=page_send.at[0, g],
                recv_sem=page_recv.at[0, g, lane_me],
                device_id={"blk": inner},
                device_id_type=mesh_id,
            ),
            pltpu.make_async_remote_copy(
                src_ref=rope_hbm.at[kept + g, :, mine_rows],
                dst_ref=rope.at[requests + g, :, mine_rows],
                send_sem=page_send.at[1, g],
                recv_sem=page_recv.at[1, g, lane_me],
                device_id={"blk": inner},
                device_id_type=mesh_id,
            ),
        )

    stages = []
    while moved and (peers >> len(stages)) > 1:
        stages.append(peers >> (len(stages) + 1))

    def partner(j, gap):
        return j + gap * (1 - 2 * lax.rem(j // gap, 2))

    def held(stage):
        slices = [lane_me]
        for gap in stages[:stage]:
            slices = slices + [partner(j, gap) for j in slices]
        return slices

    def share_copies(g, stage):
        target = partner(lane_me, stages[stage])
        pieces = held(stage)
        return [
            pltpu.make_async_remote_copy(
                src_ref=view,
                dst_ref=view,
                send_sem=peer_send.at[i, g, len(pieces) - 1 + at],
                recv_sem=page_recv.at[i, g, j],
                device_id={"head": target},
                device_id_type=mesh_id,
            )
            for at, j in enumerate(pieces)
            for i, view in enumerate(
                (lat.at[requests + g, rows_of(j)], rope.at[requests + g, :, rows_of(j)])
            )
        ]

    def await_pieces(g, pieces):
        for j in pieces:
            for i, view in enumerate(
                (lat.at[requests + g, rows_of(j)], rope.at[requests + g, :, rows_of(j)])
            ):
                pltpu.make_async_remote_copy(
                    src_ref=view,
                    dst_ref=view,
                    send_sem=page_send.at[i, g],
                    recv_sem=page_recv.at[i, g, j],
                    device_id={"blk": me},
                    device_id_type=mesh_id,
                ).wait_recv()

    def share_stage(g, stage):
        pieces = held(stage)
        await_pieces(g, pieces[len(pieces) // 2 :])
        if stage < len(stages):
            for copy in share_copies(g, stage):
                copy.start()

    barrier = pltpu.get_barrier_semaphore()

    @pl.loop(1, n)
    def _(k):
        pl.semaphore_signal(
            barrier, inc=1, device_id={"blk": lax.rem(me + k, n)}, device_id_type=mesh_id
        )

    if moved:

        @pl.loop(1, peers)
        def _(k):
            pl.semaphore_signal(
                barrier,
                inc=1,
                device_id={"head": lax.rem(lane_me + k, peers)},
                device_id_type=mesh_id,
            )

    @pl.loop(0, requests)
    def _(r):
        for copy in load_copies(r):
            copy.start()

    w_copy().start()
    pl.semaphore_wait(barrier, n - 1 + (peers - 1 if moved else 0))

    def sends_on(r, side):
        ahead = me + 1 - 2 * side
        valid = jnp.logical_and(ahead >= 0, ahead < n)
        if moved:
            last = jnp.logical_or(ahead == 0, ahead == n - 1)
            valid = jnp.logical_and(valid, jnp.logical_not(jnp.logical_and(last, r >= kept)))
        return valid

    if moved:

        @pl.when(at_end)
        def _():
            @pl.loop(0, moved)
            def _(g):
                for copy in page_copies(g):
                    copy.start()

    def send_own():
        @pl.loop(0, requests)
        def _(r):
            for side in (0, 1):

                @pl.when(sends_on(r, side))
                def _():
                    own_copy(r, side).start()

    @pl.when(jnp.logical_not(at_end) if moved else me >= 0)
    def _():
        send_own()

    lane = lax.broadcasted_iota(jnp.int32, (nodes, LANES), 1)
    total = requests * nodes
    column = lax.broadcasted_iota(jnp.int32, (total, total), 1)
    row = lax.broadcasted_iota(jnp.int32, (total, total), 0)
    parent = jnp.concatenate(
        [parent_ref[r : r + 1, :] + r * nodes for r in range(requests)], axis=1
    )
    reached = jnp.where(jnp.logical_or(parent == row, row == column), 1.0, 0.0)
    for _ in range(max(nodes - 1, 1).bit_length()):
        factor = reached.astype(jnp.bfloat16)
        reached = jnp.minimum(jnp.dot(factor, factor, preferred_element_type=jnp.float32), 1.0)
    reach[...] = reached.T.reshape(requests, nodes, total)

    if moved:
        for end in (0, n - 1):

            @pl.when(me != end)
            def _():
                @pl.loop(0, moved)
                def _(g):
                    blank = parts.at[end, kept + g]
                    blank[:, :width] = jnp.zeros((nodes, width), jnp.bfloat16)
                    blank[:, width:] = jnp.where(lane < heads, NEGATIVE, 0.0).astype(jnp.bfloat16)

    def stats(scores, values):
        top = jnp.maximum(jnp.max(scores, axis=1, keepdims=True), FLOOR)
        weights = jnp.exp2(scores - top)
        summed = jnp.sum(weights, axis=1, keepdims=True)
        acc = jnp.dot(weights.astype(jnp.bfloat16), values, preferred_element_type=jnp.float32)
        return top, summed, acc

    def page_scores(q, place, r, holder):
        s = lax.dot_general(
            q[:, :dim_lat], lat[place], (((1,), (1,)), ((), ())), preferred_element_type=jnp.float32
        )
        s = s + jnp.dot(q[:, dim_lat:], rope[place], preferred_element_type=jnp.float32)
        turn = lax.rem(holder - first_ref[r] + n, n)
        live = length_ref[r] - turn * page
        slot = lax.broadcasted_iota(jnp.int32, (1, page), 1)
        return jnp.where(slot < live, s * scale, NEGATIVE)

    def finish(top, summed, acc, origin, dst):
        any_kept = summed > 0.0
        safe = jnp.where(any_kept, summed, 1.0)
        rows = (acc * jnp.where(any_kept, 1.0 / safe, 0.0)).astype(jnp.bfloat16)
        lse = jnp.where(any_kept, top + jnp.log2(safe), NEGATIVE)
        stat = jnp.zeros((nodes, LANES), jnp.float32)
        for h in range(heads):
            span = slice(h * nodes, (h + 1) * nodes)
            projected = jnp.dot(
                rows[span], w[origin * heads + h], preferred_element_type=jnp.float32
            )
            dst[:, h * dim_v : (h + 1) * dim_v] = projected.astype(jnp.bfloat16)
            stat = jnp.where(lane % heads == h, lse[span], stat)
        high = stat.astype(jnp.bfloat16)
        rest = stat - high.astype(jnp.float32)
        middle = rest.astype(jnp.bfloat16)
        low = (rest - middle.astype(jnp.float32)).astype(jnp.bfloat16)
        packed = jnp.where(
            lane < heads,
            high.astype(jnp.float32),
            jnp.where(lane < 2 * heads, middle.astype(jnp.float32), low.astype(jnp.float32)),
        )
        dst[:, width : width + LANES] = packed.astype(jnp.bfloat16)

    w_copy().wait()

    @pl.loop(0, requests)
    def _(r):
        for copy in load_copies(r):
            copy.wait()
        q = qbuf[me, r].T
        keys = tree_ref[...].reshape(total, tree_ref.shape[2])
        s = lax.dot_general(q, keys, (((1,), (1,)), ((), ())), preferred_element_type=jnp.float32)
        seen = jnp.concatenate([reach[r]] * heads, axis=0) > 0.5
        s = jnp.where(seen, s * scale, NEGATIVE)
        top, summed, acc = stats(s, keys[:, :dim_lat])
        finish(top, summed, acc, me, parts.at[me, r])

    flipped = jnp.where(2 * me < n, 1, 0)

    def place(u, first, count):
        t = jnp.maximum(u - count, 0)
        own = u < count
        d = t // (2 * count) + 1
        side = lax.rem(t // count + flipped, 2)
        r = first + lax.rem(u, count)
        origin = jnp.where(own, me, me - d + 2 * d * side)
        valid = jnp.logical_and(origin >= 0, origin < n)
        if first:
            valid = jnp.logical_and(valid, jnp.logical_or(own, jnp.logical_not(at_end)))
        return origin, r, side, jnp.logical_not(own), valid

    classes = [(0, kept)] + ([(kept, moved)] if moved else [])

    def events(first, u):
        if not moved:
            return
        if first:

            @pl.when(jnp.logical_and(near_end, u == 0))
            def _():
                for stage in range(2, len(stages) + 1):
                    for g in range(moved):
                        share_stage(g, stage)
                if len(stages) == 1:
                    for g in range(moved):
                        share_stage(g, 1)

            return

        @pl.when(jnp.logical_and(at_end, u == kept))
        def _():
            @pl.loop(0, moved)
            def _(g):
                for copy in page_copies(g):
                    copy.wait_send()

            send_own()

        @pl.when(jnp.logical_and(near_end, u == kept + 1))
        def _():
            share_stage(0, 0)

        @pl.when(jnp.logical_and(near_end, u == 2 * kept))
        def _():
            for g in range(1, moved):
                share_stage(g, 0)
            if len(stages) > 1:
                share_stage(0, 1)

        @pl.when(jnp.logical_and(near_end, u == 3 * kept))
        def _():
            if len(stages) > 1:
                for g in range(1, moved):
                    share_stage(g, 1)

    for first, count in classes:

        @pl.loop(0, count * (2 * n - 1))
        def _(u):
            origin, r, side, foreign, valid = place(u, first, count)
            events(first, u)

            @pl.when(jnp.logical_and(foreign, valid))
            def _():
                hop_copy(origin, r, side).wait_recv()

                @pl.when(sends_on(r, side))
                def _():
                    hop_copy(origin, r, side).start()

            @pl.when(valid)
            def _():
                q = qbuf[origin, r].T
                top, summed, acc = stats(page_scores(q, r, r, me), lat[r])
                if first:
                    top_ref[...] = top
                    sum_ref[...] = summed
                    acc_ref[...] = acc

                    @pl.when(jnp.logical_and(near_end, origin != end_side))
                    def _():
                        extra = r + moved
                        top_x, sum_x, acc_x = stats(page_scores(q, extra, r, end_side), lat[extra])
                        top_a = top_ref[...]
                        both = jnp.maximum(top_a, top_x)
                        f_a, f_x = jnp.exp2(top_a - both), jnp.exp2(top_x - both)
                        top_ref[...] = both
                        sum_ref[...] = sum_ref[...] * f_a + sum_x * f_x
                        acc_ref[...] = acc_ref[...] * f_a + acc_x * f_x

                    top, summed, acc = top_ref[...], sum_ref[...], acc_ref[...]

                finish(top, summed, acc, origin, mine.at[origin, r])

                @pl.when(foreign)
                def _():
                    part_copy(origin, r, me).start()

    def arrives(r, holder):
        if not moved:
            return None
        last = jnp.logical_or(holder == 0, holder == n - 1)
        return jnp.logical_not(jnp.logical_and(last, r >= kept))

    eye = lax.broadcasted_iota(jnp.int32, (nodes, nodes), 0) == lax.broadcasted_iota(
        jnp.int32, (nodes, nodes), 1
    )

    @pl.loop(0, requests)
    def _(r):
        @pl.loop(1, n)
        def _(k):
            holder = lax.rem(me + k, n)
            if moved:

                @pl.when(arrives(r, holder))
                def _():
                    part_copy(me, r, holder).wait_recv()

            else:
                part_copy(me, r, holder).wait_recv()

        def lse_of(stat):
            stat = stat.astype(jnp.float32)
            lse = stat + pltpu.roll(stat, LANES - heads, 1) + pltpu.roll(stat, LANES - 2 * heads, 1)
            return jnp.where(lane < heads, lse, NEGATIVE)

        own = mine[me, r]
        own_lse = lse_of(own[:, width:])
        top = lax.fori_loop(
            0,
            n,
            lambda k, best: jnp.maximum(best, lse_of(parts[k, r, :, width : width + LANES])),
            own_lse,
            unroll=n <= 8,
        )
        top = jnp.where(lane < heads, top, 0.0)

        def add(carried, lse, part):
            weight_sum, summed = carried
            weight = jnp.exp2(lse - top)
            spread = jnp.concatenate(
                [jnp.broadcast_to(weight[:, h : h + 1], (nodes, dim_v)) for h in range(heads)], axis=1
            )
            return weight_sum + spread, summed + spread * part.astype(jnp.float32)

        zero = jnp.zeros((nodes, width), jnp.float32)
        weight_sum, summed = lax.fori_loop(
            0,
            n,
            lambda k, carried: add(
                carried, lse_of(parts[k, r, :, width : width + LANES]), parts[k, r, :, :width]
            ),
            add((zero, zero), own_lse, own[:, :width]),
            unroll=n <= 8,
        )
        alive = alive_ref[pl.ds(r, 1), :].astype(jnp.float32)
        alive = jnp.sum(jnp.where(eye, alive, 0.0), axis=1, keepdims=True)
        out_ref[r] = (summed / weight_sum * alive).astype(out_ref.dtype)

    if moved:

        @pl.when(near_end)
        def _():
            @pl.loop(0, moved)
            def _(g):
                for stage in range(len(stages)):
                    for copy in share_copies(g, stage):
                        copy.wait_send()

    @pl.loop(0, requests)
    def _(r):
        for side in (0, 1):

            @pl.when(sends_on(r, side))
            def _():
                own_copy(r, side).wait_send()

    for first, count in classes:

        @pl.loop(0, count * (2 * n - 1))
        def _(u):
            origin, r, side, foreign, valid = place(u, first, count)

            @pl.when(jnp.logical_and(foreign, valid))
            def _():
                @pl.when(sends_on(r, side))
                def _():
                    hop_copy(origin, r, side).wait_send()

                part_copy(origin, r, me).wait_send()


def shards(
    queries,
    tree_keys,
    parents,
    node_live,
    lengths,
    start_device,
    cache_latent,
    cache_rope,
    up_weight,
):
    n = lax.axis_size("blk")
    requests, dim_q, cols = queries.shape
    nodes = tree_keys.shape[1]
    _, page, dim_lat = cache_latent.shape
    dim_rope = cache_rope.shape[1]
    dim_v = up_weight.shape[2]
    width = cols // nodes * dim_v
    bf16 = jnp.bfloat16
    scale = math.log2(math.e) / math.sqrt(DN + dim_rope)
    peers = lax.axis_size("head")
    movable = n >= 4 and peers & (peers - 1) == 0 < peers - 1 and page % (peers * LANES) == 0
    moved = max(requests // 4, 1) if movable else 0
    slots = max(moved, 1)
    vmem = pl.BlockSpec(memory_space=pltpu.VMEM)
    smem = pl.BlockSpec(memory_space=pltpu.SMEM)
    anywhere = pl.BlockSpec(memory_space=pl.ANY)
    return pl.pallas_call(
        functools.partial(kernel, n, peers, moved, scale),
        out_shape=jax.ShapeDtypeStruct((requests, nodes, width), bf16),
        in_specs=[anywhere, vmem, vmem, vmem, smem, smem, anywhere, anywhere, anywhere],
        out_specs=vmem,
        scratch_shapes=[
            pltpu.VMEM((n, requests, dim_q, cols), bf16),
            pltpu.VMEM((requests + moved, page, dim_lat), bf16),
            pltpu.VMEM((requests + moved, dim_rope, page), bf16),
            pltpu.VMEM(up_weight.shape, bf16),
            pltpu.VMEM((n, requests, nodes, width + LANES), bf16),
            pltpu.VMEM((n, requests, nodes, width + LANES), bf16),
            pltpu.VMEM((requests, nodes, requests * nodes), jnp.float32),
            pltpu.VMEM((cols, 1), jnp.float32),
            pltpu.VMEM((cols, 1), jnp.float32),
            pltpu.VMEM((cols, dim_lat), jnp.float32),
            pltpu.SemaphoreType.DMA((3, requests)),
            pltpu.SemaphoreType.DMA,
            pltpu.SemaphoreType.DMA((2, n, requests)),
            pltpu.SemaphoreType.DMA((n, requests)),
            pltpu.SemaphoreType.DMA((n, requests)),
            pltpu.SemaphoreType.DMA((n, requests)),
            pltpu.SemaphoreType.DMA((2, slots)),
            pltpu.SemaphoreType.DMA((2, slots, peers)),
            pltpu.SemaphoreType.DMA((2, slots, peers)),
        ],
        compiler_params=pltpu.CompilerParams(
            collective_id=0, has_side_effects=True, vmem_limit_bytes=60 * 1024 * 1024
        ),
        name="tree_attention",
    )(
        queries,
        tree_keys,
        parents,
        node_live,
        lengths,
        start_device,
        cache_latent,
        cache_rope,
        up_weight,
    )


def solution(mesh):
    return jax.shard_map(
        shards,
        mesh=mesh,
        in_specs=(
            P("grp", None, ("head", "blk")),
            P("grp", None, None),
            P("grp", None),
            P("grp", None),
            P("grp"),
            P("grp"),
            P("grp", "blk", None),
            P("grp", None, "blk"),
            P("head", None, None),
        ),
        out_specs=P("grp", None, ("head", "blk")),
        check_vma=False,
    )
```

```python
import functools
import math

import jax
import jax.numpy as jnp
from jax import lax
from jax.experimental import pallas as pl
from jax.experimental.pallas import tpu as pltpu
from jax.sharding import PartitionSpec as P

DN = 128
NEGATIVE = -1e30
FLOOR = -1e29
LANES = 128


def kernel(
    n,
    peers,
    moved,
    scale,
    q_hbm,
    tree_ref,
    parent_ref,
    alive_ref,
    length_ref,
    first_ref,
    lat_hbm,
    rope_hbm,
    w_hbm,
    out_ref,
    qbuf,
    lat,
    rope,
    w,
    parts,
    mine,
    reach,
    top_ref,
    sum_ref,
    acc_ref,
    load_sem,
    w_sem,
    q_send,
    q_recv,
    p_send,
    p_recv,
    page_send,
    peer_send,
    page_recv,
):
    me = lax.axis_index("blk")
    lane_me = lax.axis_index("head")
    requests, _, cols = q_hbm.shape
    nodes = tree_ref.shape[1]
    dim_lat = lat.shape[2]
    page = lat.shape[1]
    dim_v = w.shape[2]
    heads = cols // nodes
    width = heads * dim_v
    kept = requests - moved
    share = page // peers
    mesh_id = pl.DeviceIdType.MESH
    at_end = jnp.logical_or(me == 0, me == n - 1)
    near_end = jnp.logical_or(me == 1, me == n - 2)
    end_side = jnp.where(me <= 1, 0, n - 1)

    def load_copies(r):
        return (
            pltpu.make_async_copy(q_hbm.at[r], qbuf.at[me, r], load_sem.at[0, r]),
            pltpu.make_async_copy(lat_hbm.at[r], lat.at[r], load_sem.at[1, r]),
            pltpu.make_async_copy(rope_hbm.at[r], rope.at[r], load_sem.at[2, r]),
        )

    def w_copy():
        return pltpu.make_async_copy(w_hbm, w, w_sem)

    def own_copy(r, side):
        return pltpu.make_async_remote_copy(
            src_ref=q_hbm.at[r],
            dst_ref=qbuf.at[me, r],
            send_sem=q_send.at[side, me, r],
            recv_sem=q_recv.at[me, r],
            device_id={"blk": me + 1 - 2 * side},
            device_id_type=mesh_id,
        )

    def hop_copy(origin, r, side):
        return pltpu.make_async_remote_copy(
            src_ref=qbuf.at[origin, r],
            dst_ref=qbuf.at[origin, r],
            send_sem=q_send.at[side, origin, r],
            recv_sem=q_recv.at[origin, r],
            device_id={"blk": me + 1 - 2 * side},
            device_id_type=mesh_id,
        )

    def part_copy(origin, r, holder):
        return pltpu.make_async_remote_copy(
            src_ref=mine.at[origin, r],
            dst_ref=parts.at[holder, r],
            send_sem=p_send.at[origin, r],
            recv_sem=p_recv.at[holder, r],
            device_id={"blk": origin},
            device_id_type=mesh_id,
        )

    def rows_of(j):
        return pl.ds(pl.multiple_of(j * share, share), share)

    def page_copies(g):
        inner = jnp.where(me == 0, 1, n - 2)
        mine_rows = rows_of(lane_me)
        return (
            pltpu.make_async_remote_copy(
                src_ref=lat_hbm.at[kept + g, mine_rows],
                dst_ref=lat.at[requests + g, mine_rows],
                send_sem=page_send.at[0, g],
                recv_sem=page_recv.at[0, g, lane_me],
                device_id={"blk": inner},
                device_id_type=mesh_id,
            ),
            pltpu.make_async_remote_copy(
                src_ref=rope_hbm.at[kept + g, :, mine_rows],
                dst_ref=rope.at[requests + g, :, mine_rows],
                send_sem=page_send.at[1, g],
                recv_sem=page_recv.at[1, g, lane_me],
                device_id={"blk": inner},
                device_id_type=mesh_id,
            ),
        )

    stages = []
    while moved and (peers >> len(stages)) > 1:
        stages.append(peers >> (len(stages) + 1))

    def partner(j, gap):
        return j + gap * (1 - 2 * lax.rem(j // gap, 2))

    def held(stage):
        slices = [lane_me]
        for gap in stages[:stage]:
            slices = slices + [partner(j, gap) for j in slices]
        return slices

    def share_copies(g, stage):
        target = partner(lane_me, stages[stage])
        pieces = held(stage)
        return [
            pltpu.make_async_remote_copy(
                src_ref=view,
                dst_ref=view,
                send_sem=peer_send.at[i, g, len(pieces) - 1 + at],
                recv_sem=page_recv.at[i, g, j],
                device_id={"head": target},
                device_id_type=mesh_id,
            )
            for at, j in enumerate(pieces)
            for i, view in enumerate(
                (lat.at[requests + g, rows_of(j)], rope.at[requests + g, :, rows_of(j)])
            )
        ]

    def await_pieces(g, pieces):
        for j in pieces:
            for i, view in enumerate(
                (lat.at[requests + g, rows_of(j)], rope.at[requests + g, :, rows_of(j)])
            ):
                pltpu.make_async_remote_copy(
                    src_ref=view,
                    dst_ref=view,
                    send_sem=page_send.at[i, g],
                    recv_sem=page_recv.at[i, g, j],
                    device_id={"blk": me},
                    device_id_type=mesh_id,
                ).wait_recv()

    def share_stage(g, stage):
        pieces = held(stage)
        await_pieces(g, pieces[len(pieces) // 2 :])
        if stage < len(stages):
            for copy in share_copies(g, stage):
                copy.start()

    barrier = pltpu.get_barrier_semaphore()

    @pl.loop(1, n)
    def _(k):
        pl.semaphore_signal(
            barrier, inc=1, device_id={"blk": lax.rem(me + k, n)}, device_id_type=mesh_id
        )

    if moved:

        @pl.loop(1, peers)
        def _(k):
            pl.semaphore_signal(
                barrier,
                inc=1,
                device_id={"head": lax.rem(lane_me + k, peers)},
                device_id_type=mesh_id,
            )

    @pl.loop(0, requests)
    def _(r):
        for copy in load_copies(r):
            copy.start()

    w_copy().start()
    pl.semaphore_wait(barrier, n - 1 + (peers - 1 if moved else 0))

    def sends_on(r, side):
        ahead = me + 1 - 2 * side
        valid = jnp.logical_and(ahead >= 0, ahead < n)
        if moved:
            last = jnp.logical_or(ahead == 0, ahead == n - 1)
            valid = jnp.logical_and(valid, jnp.logical_not(jnp.logical_and(last, r >= kept)))
        return valid

    if moved:

        @pl.when(at_end)
        def _():
            @pl.loop(0, moved)
            def _(g):
                for copy in page_copies(g):
                    copy.start()

    def send_own():
        @pl.loop(0, requests)
        def _(r):
            for side in (0, 1):

                @pl.when(sends_on(r, side))
                def _():
                    own_copy(r, side).start()

    @pl.when(jnp.logical_not(at_end) if moved else me >= 0)
    def _():
        send_own()

    lane = lax.broadcasted_iota(jnp.int32, (nodes, LANES), 1)
    total = requests * nodes
    column = lax.broadcasted_iota(jnp.int32, (total, total), 1)
    row = lax.broadcasted_iota(jnp.int32, (total, total), 0)
    parent = jnp.concatenate(
        [parent_ref[r : r + 1, :] + r * nodes for r in range(requests)], axis=1
    )
    reached = jnp.where(jnp.logical_or(parent == row, row == column), 1.0, 0.0)
    for _ in range(max(nodes - 1, 1).bit_length()):
        factor = reached.astype(jnp.bfloat16)
        reached = jnp.minimum(jnp.dot(factor, factor, preferred_element_type=jnp.float32), 1.0)
    reach[...] = reached.T.reshape(requests, nodes, total)

    if moved:
        for end in (0, n - 1):

            @pl.when(me != end)
            def _():
                @pl.loop(0, moved)
                def _(g):
                    blank = parts.at[end, kept + g]
                    blank[:, :width] = jnp.zeros((nodes, width), jnp.bfloat16)
                    blank[:, width:] = jnp.where(lane < heads, NEGATIVE, 0.0).astype(jnp.bfloat16)

    def stats(scores, values):
        top = jnp.maximum(jnp.max(scores, axis=1, keepdims=True), FLOOR)
        weights = jnp.exp2(scores - top)
        summed = jnp.sum(weights, axis=1, keepdims=True)
        acc = jnp.dot(weights.astype(jnp.bfloat16), values, preferred_element_type=jnp.float32)
        return top, summed, acc

    def page_scores(q, place, r, holder):
        s = lax.dot_general(
            q[:, :dim_lat], lat[place], (((1,), (1,)), ((), ())), preferred_element_type=jnp.float32
        )
        s = s + jnp.dot(q[:, dim_lat:], rope[place], preferred_element_type=jnp.float32)
        turn = lax.rem(holder - first_ref[r] + n, n)
        live = length_ref[r] - turn * page
        slot = lax.broadcasted_iota(jnp.int32, (1, page), 1)
        return jnp.where(slot < live, s * scale, NEGATIVE)

    def finish(top, summed, acc, origin, dst):
        any_kept = summed > 0.0
        safe = jnp.where(any_kept, summed, 1.0)
        rows = (acc * jnp.where(any_kept, 1.0 / safe, 0.0)).astype(jnp.bfloat16)
        lse = jnp.where(any_kept, top + jnp.log2(safe), NEGATIVE)
        stat = jnp.zeros((nodes, LANES), jnp.float32)
        for h in range(heads):
            span = slice(h * nodes, (h + 1) * nodes)
            projected = jnp.dot(
                rows[span], w[origin * heads + h], preferred_element_type=jnp.float32
            )
            dst[:, h * dim_v : (h + 1) * dim_v] = projected.astype(jnp.bfloat16)
            stat = jnp.where(lane % heads == h, lse[span], stat)
        high = stat.astype(jnp.bfloat16)
        rest = stat - high.astype(jnp.float32)
        middle = rest.astype(jnp.bfloat16)
        low = (rest - middle.astype(jnp.float32)).astype(jnp.bfloat16)
        packed = jnp.where(
            lane < heads,
            high.astype(jnp.float32),
            jnp.where(lane < 2 * heads, middle.astype(jnp.float32), low.astype(jnp.float32)),
        )
        dst[:, width : width + LANES] = packed.astype(jnp.bfloat16)

    w_copy().wait()

    @pl.loop(0, requests)
    def _(r):
        for copy in load_copies(r):
            copy.wait()
        q = qbuf[me, r].T
        keys = tree_ref[...].reshape(total, tree_ref.shape[2])
        s = lax.dot_general(q, keys, (((1,), (1,)), ((), ())), preferred_element_type=jnp.float32)
        seen = jnp.concatenate([reach[r]] * heads, axis=0) > 0.5
        s = jnp.where(seen, s * scale, NEGATIVE)
        top, summed, acc = stats(s, keys[:, :dim_lat])
        finish(top, summed, acc, me, parts.at[me, r])

    flipped = jnp.where(2 * me < n, 1, 0)

    def place(u, first, count):
        t = jnp.maximum(u - count, 0)
        own = u < count
        d = t // (2 * count) + 1
        side = lax.rem(t // count + flipped, 2)
        r = first + lax.rem(u, count)
        origin = jnp.where(own, me, me - d + 2 * d * side)
        valid = jnp.logical_and(origin >= 0, origin < n)
        if first:
            valid = jnp.logical_and(valid, jnp.logical_or(own, jnp.logical_not(at_end)))
        return origin, r, side, jnp.logical_not(own), valid

    classes = [(0, kept)] + ([(kept, moved)] if moved else [])

    def events(first, u):
        if not moved:
            return
        if first:

            @pl.when(jnp.logical_and(near_end, u == 0))
            def _():
                for stage in range(2, len(stages) + 1):
                    for g in range(moved):
                        share_stage(g, stage)
                if len(stages) == 1:
                    for g in range(moved):
                        share_stage(g, 1)

            return

        @pl.when(jnp.logical_and(at_end, u == kept))
        def _():
            @pl.loop(0, moved)
            def _(g):
                for copy in page_copies(g):
                    copy.wait_send()

            send_own()

        @pl.when(jnp.logical_and(near_end, u == kept + 1))
        def _():
            share_stage(0, 0)

        @pl.when(jnp.logical_and(near_end, u == 2 * kept))
        def _():
            for g in range(1, moved):
                share_stage(g, 0)
            if len(stages) > 1:
                share_stage(0, 1)

        @pl.when(jnp.logical_and(near_end, u == 3 * kept))
        def _():
            if len(stages) > 1:
                for g in range(1, moved):
                    share_stage(g, 1)

    def pass_on(origin, r, side):
        hop_copy(origin, r, side).wait_recv()

        @pl.when(sends_on(r, side))
        def _():
            hop_copy(origin, r, side).start()

    for first, count in classes:

        @pl.loop(0, count * (2 * n - 1))
        def _(u):
            origin, r, side, foreign, valid = place(u, first, count)
            events(first, u)

            if moved and not first:

                @pl.when(u == 4 * kept)
                def _():
                    @pl.loop(moved, 3 * moved)
                    def _(later):
                        origin_l, r_l, side_l, _, valid_l = place(later, kept, moved)

                        @pl.when(valid_l)
                        def _():
                            pass_on(origin_l, r_l, side_l)

            fresh = jnp.logical_and(foreign, u >= 3 * count) if first else foreign

            @pl.when(jnp.logical_and(fresh, valid))
            def _():
                pass_on(origin, r, side)

            @pl.when(valid)
            def _():
                q = qbuf[origin, r].T
                top, summed, acc = stats(page_scores(q, r, r, me), lat[r])
                if first:
                    top_ref[...] = top
                    sum_ref[...] = summed
                    acc_ref[...] = acc

                    @pl.when(jnp.logical_and(near_end, origin != end_side))
                    def _():
                        extra = r + moved
                        top_x, sum_x, acc_x = stats(page_scores(q, extra, r, end_side), lat[extra])
                        top_a = top_ref[...]
                        both = jnp.maximum(top_a, top_x)
                        f_a, f_x = jnp.exp2(top_a - both), jnp.exp2(top_x - both)
                        top_ref[...] = both
                        sum_ref[...] = sum_ref[...] * f_a + sum_x * f_x
                        acc_ref[...] = acc_ref[...] * f_a + acc_x * f_x

                    top, summed, acc = top_ref[...], sum_ref[...], acc_ref[...]

                finish(top, summed, acc, origin, mine.at[origin, r])

                @pl.when(foreign)
                def _():
                    part_copy(origin, r, me).start()

    def arrives(r, holder):
        if not moved:
            return None
        last = jnp.logical_or(holder == 0, holder == n - 1)
        return jnp.logical_not(jnp.logical_and(last, r >= kept))

    eye = lax.broadcasted_iota(jnp.int32, (nodes, nodes), 0) == lax.broadcasted_iota(
        jnp.int32, (nodes, nodes), 1
    )

    @pl.loop(0, requests)
    def _(r):
        @pl.loop(1, n)
        def _(k):
            holder = lax.rem(me + k, n)
            if moved:

                @pl.when(arrives(r, holder))
                def _():
                    part_copy(me, r, holder).wait_recv()

            else:
                part_copy(me, r, holder).wait_recv()

        def lse_of(stat):
            stat = stat.astype(jnp.float32)
            lse = stat + pltpu.roll(stat, LANES - heads, 1) + pltpu.roll(stat, LANES - 2 * heads, 1)
            return jnp.where(lane < heads, lse, NEGATIVE)

        own = mine[me, r]
        own_lse = lse_of(own[:, width:])
        top = lax.fori_loop(
            0,
            n,
            lambda k, best: jnp.maximum(best, lse_of(parts[k, r, :, width : width + LANES])),
            own_lse,
            unroll=n <= 8,
        )
        top = jnp.where(lane < heads, top, 0.0)

        def add(carried, lse, part):
            weight_sum, summed = carried
            weight = jnp.exp2(lse - top)
            spread = jnp.concatenate(
                [jnp.broadcast_to(weight[:, h : h + 1], (nodes, dim_v)) for h in range(heads)], axis=1
            )
            return weight_sum + spread, summed + spread * part.astype(jnp.float32)

        zero = jnp.zeros((nodes, width), jnp.float32)
        weight_sum, summed = lax.fori_loop(
            0,
            n,
            lambda k, carried: add(
                carried, lse_of(parts[k, r, :, width : width + LANES]), parts[k, r, :, :width]
            ),
            add((zero, zero), own_lse, own[:, :width]),
            unroll=n <= 8,
        )
        alive = alive_ref[pl.ds(r, 1), :].astype(jnp.float32)
        alive = jnp.sum(jnp.where(eye, alive, 0.0), axis=1, keepdims=True)
        out_ref[r] = (summed / weight_sum * alive).astype(out_ref.dtype)

    if moved:

        @pl.when(near_end)
        def _():
            @pl.loop(0, moved)
            def _(g):
                for stage in range(len(stages)):
                    for copy in share_copies(g, stage):
                        copy.wait_send()

    @pl.loop(0, requests)
    def _(r):
        for side in (0, 1):

            @pl.when(sends_on(r, side))
            def _():
                own_copy(r, side).wait_send()

    for first, count in classes:

        @pl.loop(0, count * (2 * n - 1))
        def _(u):
            origin, r, side, foreign, valid = place(u, first, count)

            @pl.when(jnp.logical_and(foreign, valid))
            def _():
                @pl.when(sends_on(r, side))
                def _():
                    hop_copy(origin, r, side).wait_send()

                part_copy(origin, r, me).wait_send()


def shards(
    queries,
    tree_keys,
    parents,
    node_live,
    lengths,
    start_device,
    cache_latent,
    cache_rope,
    up_weight,
):
    n = lax.axis_size("blk")
    requests, dim_q, cols = queries.shape
    nodes = tree_keys.shape[1]
    _, page, dim_lat = cache_latent.shape
    dim_rope = cache_rope.shape[1]
    dim_v = up_weight.shape[2]
    width = cols // nodes * dim_v
    bf16 = jnp.bfloat16
    scale = math.log2(math.e) / math.sqrt(DN + dim_rope)
    peers = lax.axis_size("head")
    movable = n >= 4 and peers & (peers - 1) == 0 < peers - 1 and page % (peers * LANES) == 0
    moved = requests // 2 if movable else 0
    slots = max(moved, 1)
    vmem = pl.BlockSpec(memory_space=pltpu.VMEM)
    smem = pl.BlockSpec(memory_space=pltpu.SMEM)
    anywhere = pl.BlockSpec(memory_space=pl.ANY)
    return pl.pallas_call(
        functools.partial(kernel, n, peers, moved, scale),
        out_shape=jax.ShapeDtypeStruct((requests, nodes, width), bf16),
        in_specs=[anywhere, vmem, vmem, vmem, smem, smem, anywhere, anywhere, anywhere],
        out_specs=vmem,
        scratch_shapes=[
            pltpu.VMEM((n, requests, dim_q, cols), bf16),
            pltpu.VMEM((requests + moved, page, dim_lat), bf16),
            pltpu.VMEM((requests + moved, dim_rope, page), bf16),
            pltpu.VMEM(up_weight.shape, bf16),
            pltpu.VMEM((n, requests, nodes, width + LANES), bf16),
            pltpu.VMEM((n, requests, nodes, width + LANES), bf16),
            pltpu.VMEM((requests, nodes, requests * nodes), jnp.float32),
            pltpu.VMEM((cols, 1), jnp.float32),
            pltpu.VMEM((cols, 1), jnp.float32),
            pltpu.VMEM((cols, dim_lat), jnp.float32),
            pltpu.SemaphoreType.DMA((3, requests)),
            pltpu.SemaphoreType.DMA,
            pltpu.SemaphoreType.DMA((2, n, requests)),
            pltpu.SemaphoreType.DMA((n, requests)),
            pltpu.SemaphoreType.DMA((n, requests)),
            pltpu.SemaphoreType.DMA((n, requests)),
            pltpu.SemaphoreType.DMA((2, slots)),
            pltpu.SemaphoreType.DMA((2, slots, peers)),
            pltpu.SemaphoreType.DMA((2, slots, peers)),
        ],
        compiler_params=pltpu.CompilerParams(
            collective_id=0, has_side_effects=True, vmem_limit_bytes=60 * 1024 * 1024
        ),
        name="tree_attention",
    )(
        queries,
        tree_keys,
        parents,
        node_live,
        lengths,
        start_device,
        cache_latent,
        cache_rope,
        up_weight,
    )


def solution(mesh):
    return jax.shard_map(
        shards,
        mesh=mesh,
        in_specs=(
            P("grp", None, ("head", "blk")),
            P("grp", None, None),
            P("grp", None),
            P("grp", None),
            P("grp"),
            P("grp"),
            P("grp", "blk", None),
            P("grp", None, "blk"),
            P("head", None, None),
        ),
        out_specs=P("grp", None, ("head", "blk")),
        check_vma=False,
    )
```
